512 devices in a mesh: sec: 2 (over core), grp: 16 (over y_hi, x), dev: 16 (over y_lo, z).
Axes of the slice: x: 4, y: 8 (y_hi: 4, y_lo: 2; y = y_hi * 2 + y_lo), z: 8, core: 2. Of those that a mesh axis runs over, the one named last changes fastest.
Arguments:
- q_latent: bfloat16 [256, 128, 512], P(('grp', 'dev')), may hold values from -16 to 16
- q_rope: bfloat16 [256, 8192], P(('grp', 'dev')), may hold values from -6 to 6
- cache_latent: bfloat16 [256, 2048, 512], P(('grp', 'dev'), 'sec'), may hold values from -6 to 6
- cache_rope: bfloat16 [256, 64, 2048], P(('grp', 'dev'), None, 'sec'), may hold values from -6 to 6
- lengths: int32 [256], P(('grp', 'dev')), may hold values from 2 to 2048
- w_uv: bfloat16 [128, 512, 128], P(('sec', 'grp')), may hold values from -1 to 1
- w_out: bfloat16 [16384, 7168], P(('sec', 'grp'), 'dev'), may hold values from -0.046875 to 0.046875
- resid: bfloat16 [256, 7168], P(('sec', 'grp'), 'dev'), may hold values from -6 to 6
- norm_gain: float32 [7168], P('dev'), may hold values from 0.1 to 1.9
- router: float32 [7168, 16], P('dev'), may hold values from -0.0625 to 0.0625
- routes: int32 [256, 8], P(('sec', 'grp')), may hold values from 0 to 15, as said below
- slots: int32 [256, 8], P(('sec', 'grp')), may hold values from 0 to 7, as said below
- w_gateup: bfloat16 [16, 7168, 2, 2048], P('grp', 'dev', None, 'sec'), may hold values from -0.0625 to 0.0625
- w_down: bfloat16 [16, 2048, 7168], P('grp', 'sec', 'dev'), may hold values from -0.125 to 0.125
Outputs:
- layer_out: bfloat16 [256, 7168], P(('sec', 'grp'), 'dev')
The draws below stay inside these ranges and needn't reach their ends.
Inputs may be any that keep to these rules, and one draw needn't show every extreme that they name: `routes`: each row names 8 different experts; one expert is named by every row. Within each aligned block of 8 rows, the routes that name one expert hold the slots 0, 1, ... up to their number less one, each once.
All inputs are finite; a program needn't handle non-finite values.
Results may differ from the reference program's by a relative error of at most 0.033.
Values may be sent and summed in bfloat16 or wider, within the bound.
No kernel may reach another device: no remote copies, remote signals or barrier semaphores. Data moves between devices by JAX's collectives and lax.ppermute only.
A program may use at most 64 MiB of HBM per device.

```python
import jax
import jax.numpy as jnp
from jax import lax

D = 7168
H = 128
LAT = 512
ROPE = 64
VD = 128
FF = 2048
HIST_DEV = 1024
HIST = 2048
ROWS = 256
BLOCK = 8
CAP = 6
EXPERTS = 16
TOPK = 8
N_SEC = 2
N_DEV = 16


def latent_entries(key, row_ids, position_ids):

    def one_entry(row_id, position_id):
        return jax.random.normal(jax.random.fold_in(key, row_id * HIST + position_id), (LAT,), jnp.float32)
    per_position = jax.vmap(one_entry, (None, 0))
    return jax.vmap(per_position, (0, None))(row_ids, position_ids)


def draw_cache_latent(key, part):
    entries = latent_entries(jax.random.fold_in(key, 7), jnp.arange(ROWS, dtype=jnp.int32), jnp.arange(HIST, dtype=jnp.int32))
    entries = jnp.clip(entries, -6.0, 6.0)
    return entries.astype(jnp.bfloat16)


def draw_q_latent(key, part):
    key_pair = jnp.sign(latent_entries(jax.random.fold_in(key, 7), jnp.arange(ROWS, dtype=jnp.int32), jnp.arange(2, dtype=jnp.int32)))
    row_index = jnp.arange(ROWS, dtype=jnp.int32)[:, None]
    head_index = jnp.arange(H, dtype=jnp.int32)[None, :]
    picked = (row_index * 3 + head_index) % 7 == 0
    strength = 4.0 + 2.0 * ((row_index + head_index) % 3).astype(jnp.float32)
    background = jnp.clip(jax.random.normal(jax.random.fold_in(key, 11), (ROWS, H, LAT), jnp.float32), -6.0, 6.0)
    aligned = strength[:, :, None] * key_pair[:, None, 0, :]
    entries = jnp.where(picked[:, :, None], aligned, background)
    return entries.astype(jnp.bfloat16)


def route_table(key):
    noise = jax.random.randint(jax.random.fold_in(key, 101), (ROWS, EXPERTS), 0, 1 << 20)
    favour = jax.random.randint(jax.random.fold_in(key, 102), (EXPERTS,), 0, 1 << 20)
    hottest = jax.random.randint(jax.random.fold_in(key, 103), (), 0, EXPERTS)
    expert_ids = jnp.arange(EXPERTS, dtype=jnp.int32)
    boost = jnp.where(expert_ids == hottest, 1 << 22, 0)
    ranking = (noise + favour[None, :] + boost[None, :]) * EXPERTS + expert_ids[None, :]
    return lax.top_k(ranking, TOPK)[1].astype(jnp.int32)


def draw_routes(key, part):
    return route_table(key)


def draw_slots(key, part):
    table = route_table(key)
    blocks = ROWS // BLOCK
    tie_breaks = jax.random.randint(jax.random.fold_in(key, 104), (ROWS, TOPK), 0, 1 << 16)
    local_order = jnp.arange(BLOCK * TOPK, dtype=jnp.int32)
    order_key = tie_breaks.reshape(blocks, BLOCK * TOPK) * (BLOCK * TOPK) + local_order[None, :]
    flat_routes = table.reshape(blocks, BLOCK * TOPK)
    same_expert = flat_routes[:, :, None] == flat_routes[:, None, :]
    earlier = order_key[:, None, :] < order_key[:, :, None]
    slot_ranks = jnp.sum(same_expert & earlier, axis=-1).astype(jnp.int32)
    return slot_ranks.reshape(ROWS, TOPK)


def place_ends(values, stream_key, least, largest):
    longest = values.shape.index(max(values.shape))
    spots = []
    for shift in (0, 1):
        where = [jax.random.randint(jax.random.fold_in(stream_key, axis), (), 0, length) for axis, length in enumerate(values.shape)]
        where[longest] = (where[longest] + shift) % values.shape[longest]
        spots.append(tuple(where))
    return values.at[spots[0]].set(least).at[spots[1]].set(largest)


def shard_levels(stream_key, shape, cuts, low, high):
    level, own = 1.0, jax.random.fold_in(stream_key, 6)
    for axis_at, shards_of in cuts:
        draws = jnp.exp(jax.random.uniform(jax.random.fold_in(own, axis_at), (shards_of,), jnp.float32, low / len(cuts), high / len(cuts)))
        level = level * jnp.repeat(draws, shape[axis_at] // shards_of).reshape([-1 if axis == axis_at else 1 for axis in range(len(shape))])
    return level


def gaussian(stream_key, dims, deviation, limit, shards=(), kind=jnp.bfloat16):
    gain = shard_levels(stream_key, dims, shards, -0.22, 0.18) if shards else 1.0
    array = jax.random.normal(stream_key, dims, jnp.float32) * deviation * gain
    return jnp.minimum(jnp.maximum(array, -limit), limit).astype(kind)


def setup_inputs(seed: int = 0) -> dict:
    key_of = jax.random.split(jax.random.key(seed), 15)
    return {
        "q_latent": draw_q_latent(jax.random.fold_in(key_of[14], 71), 0),
        "q_rope": gaussian(key_of[1], (ROWS, H * ROPE), 1.0, 6.0, ((0, 256),)),
        "cache_latent": draw_cache_latent(jax.random.fold_in(key_of[14], 71), 0),
        "cache_rope": gaussian(key_of[3], (ROWS, ROPE, HIST), 1.0, 6.0, ((0, 256), (2, 2))),
        "lengths": place_ends(jax.random.randint(key_of[4], (ROWS,), 2, HIST + 1), jax.random.fold_in(key_of[4], 1), 2, HIST).astype(jnp.int32),
        "w_uv": gaussian(key_of[5], (H, LAT, VD), (LAT // 16) ** -0.5, 1.0, ((0, 32),)),
        "w_out": gaussian(key_of[6], (H * VD, D), (H * VD) ** -0.5, 0.046875, ((0, 32), (1, 16))),
        "resid": gaussian(key_of[7], (ROWS, D), 1.0, 6.0, ((0, 32), (1, 16))),
        "norm_gain": jnp.clip(1.0 + 0.18 * jax.random.normal(key_of[8], (D,), jnp.float32), 0.1, 1.9),
        "router": gaussian(key_of[9], (D, EXPERTS), D ** -0.5, 0.0625, ((0, 16),), jnp.float32),
        "routes": draw_routes(jax.random.fold_in(key_of[14], 71), 0),
        "slots": draw_slots(jax.random.fold_in(key_of[14], 71), 0),
        "w_gateup": gaussian(key_of[12], (EXPERTS, D, 2, FF), D ** -0.5, 0.0625, ((0, 16), (1, 16), (3, 2))),
        "w_down": gaussian(key_of[13], (EXPERTS, FF, D), FF ** -0.5, 0.125, ((0, 16), (1, 2), (2, 16))),
    }


score_scale = 0.07216878364870323
route_scale = 2.5
norm_eps = 1e-06
masked_floor = -1e+30

def attend_row(inputs):
    query_latent, query_rope, row_latent, row_rope, length = inputs
    scores = (jnp.dot(query_latent, row_latent.T, preferred_element_type=jnp.float32) + jnp.dot(query_rope, row_rope, preferred_element_type=jnp.float32)) * score_scale
    top_list = []
    mass_list = []
    weight_list = []
    for section in range(N_SEC):
        begin_at = section * HIST_DEV
        block_scores = scores[:, begin_at:begin_at + HIST_DEV]
        positions = begin_at + jnp.arange(HIST_DEV, dtype=jnp.int32)
        usable = (positions < length)[None, :]
        masked = jnp.where(usable, block_scores, masked_floor)
        top_score = lax.optimization_barrier(jnp.max(masked, axis=-1))
        expon = jnp.where(usable, jnp.exp(masked - top_score[:, None]), 0.0)
        top_list.append(top_score)
        mass_list.append(lax.optimization_barrier(jnp.sum(expon, axis=-1)))
        weight_list.append(jnp.dot(expon.astype(jnp.bfloat16), row_latent[begin_at:begin_at + HIST_DEV], preferred_element_type=jnp.float32))
    top_all = top_list[0]
    for candidate in top_list[1:]:
        top_all = jnp.maximum(top_all, candidate)
    mass_total = jnp.zeros_like(top_all)
    weighted_total = jnp.zeros_like(weight_list[0])
    for position_block in range(N_SEC):
        factor = jnp.exp(top_list[position_block] - top_all)
        mass_total = mass_total + mass_list[position_block] * factor
        weighted_total = weighted_total + weight_list[position_block] * factor[:, None]
    return (weighted_total / mass_total[:, None]).astype(jnp.bfloat16)

def expert_output(normed, gate_weight, down_weight):
    split_rows = normed.reshape(ROWS, N_DEV, D // N_DEV).astype(jnp.float32)
    split_weight = gate_weight.reshape(N_DEV, D // N_DEV, 2 * FF).astype(jnp.float32)
    partials = jnp.einsum('rkd,kdf->rkf', split_rows, split_weight, precision=lax.Precision.HIGHEST).astype(jnp.bfloat16)
    partials = lax.optimization_barrier(partials)
    gate_up = lax.optimization_barrier(jnp.sum(partials.astype(jnp.float32), axis=1)).reshape(ROWS, 2, FF)
    activated = (jax.nn.silu(gate_up[:, 0]) * gate_up[:, 1]).astype(jnp.bfloat16)
    return jnp.dot(activated, down_weight, preferred_element_type=jnp.float32).astype(jnp.bfloat16)

def reference(q_latent, q_rope, cache_latent, cache_rope, lengths, w_uv, w_out, resid, norm_gain, router, routes, slots, w_gateup, w_down):
    latent_out = lax.map(attend_row, (q_latent, q_rope.reshape(ROWS, H, ROPE), cache_latent, cache_rope, lengths))
    values = jnp.einsum('rhc,hcv->rhv', latent_out.astype(jnp.float32), w_uv.astype(jnp.float32), precision=lax.Precision.HIGHEST).astype(jnp.bfloat16)
    values = values.reshape(ROWS, H * VD)
    attention = jnp.dot(values, w_out, preferred_element_type=jnp.float32)
    hidden_state = resid.astype(jnp.float32) + attention
    inverse_rms = lax.rsqrt(lax.optimization_barrier(jnp.mean(hidden_state * hidden_state, axis=-1)) + norm_eps)
    normed_full = hidden_state * inverse_rms[:, None] * norm_gain
    normed = normed_full.astype(jnp.bfloat16)
    logits = jnp.dot(normed_full, router, precision=lax.Precision.HIGHEST)
    sigmoid_scores = jax.nn.sigmoid(logits)
    picked = jnp.take_along_axis(sigmoid_scores, routes, axis=1)
    route_weight = route_scale * picked / lax.optimization_barrier(jnp.sum(picked, axis=-1, keepdims=True))
    route_weight = jnp.where(slots < CAP, route_weight, 0.0)

    def per_expert(expert_id):
        return expert_output(normed, w_gateup[expert_id], w_down[expert_id])
    expert_out = lax.map(per_expert, jnp.arange(EXPERTS, dtype=jnp.int32))
    row_ids = jnp.arange(ROWS, dtype=jnp.int32)[:, None]
    fetched = expert_out[routes, row_ids]
    mixture = lax.optimization_barrier(jnp.sum(route_weight[:, :, None] * fetched.astype(jnp.float32), axis=1))
    return (hidden_state + mixture).astype(jnp.bfloat16)
```

```python
import jax
import jax.numpy as jnp
from jax import lax
from jax.sharding import PartitionSpec as P

score_scale = 0.07216878364870323
route_scale = 2.5
norm_eps = 1e-06
masked_floor = -1e30
f32 = jnp.float32
bf16 = jnp.bfloat16


def split_2(value):
    high = value.astype(bf16)
    low = (value - high.astype(f32)).astype(bf16)
    return high, low


def spread(value, axis):
    copies = jnp.broadcast_to(value[None], (lax.axis_size(axis),) + value.shape)
    return lax.all_to_all(copies, axis, split_axis=0, concat_axis=0, tiled=True)


def body(
    q_latent,
    q_rope,
    cache_latent,
    cache_rope,
    lengths,
    w_uv,
    w_out,
    resid,
    norm_gain,
    router,
    routes,
    slots,
    w_gateup,
    w_down,
):
    sections = lax.axis_size("sec")
    groups = lax.axis_size("grp")
    members = lax.axis_size("dev")
    section = lax.axis_index("sec")
    _, head_total, latent = q_latent.shape
    hist_local = cache_latent.shape[1]
    rope_width = cache_rope.shape[1]
    half_heads = head_total // sections
    head_block, _, value_width = w_uv.shape
    block_rows, width_local = resid.shape
    choices = routes.shape[1]
    expert_total = router.shape[1]
    capacity = max(2, 3 * block_rows // 4)
    pair_rows = sections * block_rows

    query = q_latent[0]
    rope_query = q_rope.reshape(head_total, rope_width)
    scores = (
        jnp.einsum("hc,pc->hp", query, cache_latent[0], preferred_element_type=f32)
        + jnp.einsum("hj,jp->hp", rope_query, cache_rope[0], preferred_element_type=f32)
    ) * score_scale
    positions = section * hist_local + jnp.arange(hist_local, dtype=jnp.int32)
    usable = (positions < lengths[0])[None, :]
    masked = jnp.where(usable, scores, masked_floor)
    top = jnp.max(masked, axis=-1, keepdims=True).astype(bf16)
    expon = jnp.where(usable, jnp.exp(masked - top.astype(f32)), 0.0)
    mass = jnp.sum(expon, axis=-1, keepdims=True)
    weighted = jnp.dot(expon.astype(bf16), cache_latent[0], preferred_element_type=f32)

    mass_high, mass_low = split_2(mass)
    route_part = jnp.concatenate([routes, slots], axis=1).astype(bf16)
    route_part = jnp.pad(route_part, ((0, half_heads - block_rows), (0, 0)))

    def half(value, which):
        return lax.dynamic_slice_in_dim(value, which * half_heads, half_heads, 0)

    other = 1 - section
    spare = 128 - 3 - 2 * choices
    outgoing = jnp.concatenate(
        [
            half(weighted, other).astype(bf16),
            half(top, other),
            half(mass_high, other),
            half(mass_low, other),
            route_part,
            jnp.zeros((half_heads, spare), bf16),
        ],
        axis=1,
    )
    both = lax.all_gather(outgoing, "sec", axis=0)
    theirs = lax.dynamic_index_in_dim(both, other, 0, False)
    top_mine = half(top, section).astype(f32)
    top_theirs = theirs[:, latent : latent + 1].astype(f32)
    mass_theirs = (
        theirs[:, latent + 1 : latent + 2].astype(f32)
        + theirs[:, latent + 2 : latent + 3].astype(f32)
    )
    top_both = jnp.maximum(top_mine, top_theirs)
    factor_mine = jnp.exp(top_mine - top_both)
    factor_theirs = jnp.exp(top_theirs - top_both)
    mass_both = half(mass, section) * factor_mine + mass_theirs * factor_theirs
    latent_out = (
        half(weighted, section) * factor_mine + theirs[:, :latent].astype(f32) * factor_theirs
    ) / mass_both
    latent_out = latent_out.astype(bf16)
    pair_table = both[:, :block_rows, latent + 3 : latent + 3 + 2 * choices]
    pair_table = pair_table.reshape(pair_rows, 2 * choices).astype(jnp.int32)
    pair_routes, pair_slots = pair_table[:, :choices], pair_table[:, choices:]

    outgoing_heads = latent_out.reshape(groups, head_block, latent)
    arrived = lax.all_to_all(outgoing_heads, "grp", split_axis=0, concat_axis=0, tiled=True)
    values = jnp.einsum("nhc,hcv->nhv", arrived, w_uv, preferred_element_type=f32).astype(bf16)
    width_heads = head_block * value_width
    gathered = spread(values.reshape(groups, width_heads), "dev")
    rows_by_block = gathered.transpose(1, 0, 2).reshape(sections, groups, block_rows, width_heads)
    rows_by_block = rows_by_block.transpose(1, 0, 2, 3).reshape(-1, width_heads)
    partial = jnp.dot(rows_by_block, w_out, preferred_element_type=f32).astype(bf16)
    partial = partial.reshape(groups, pair_rows, width_local)
    partial = lax.all_to_all(partial, "grp", split_axis=0, concat_axis=0, tiled=True)
    summed = jnp.sum(partial.astype(f32), axis=0).reshape(sections, block_rows, width_local)
    is_mine = (jnp.arange(sections) == section)[:, None, None]
    summed = summed + jnp.where(is_mine, resid.astype(f32)[None], 0.0)
    hidden = jnp.sum(lax.all_gather(summed, "sec", axis=0), axis=0)
    hidden_mine = lax.dynamic_index_in_dim(hidden, section, 0, False)
    hidden = hidden.reshape(pair_rows, width_local)

    gained = hidden * norm_gain
    square_high, square_low = split_2(jnp.sum(hidden * hidden, axis=-1, keepdims=True))
    logit_high, logit_low = split_2(jnp.dot(gained, router, precision=lax.Precision.HIGHEST))
    expert_ids = jnp.arange(expert_total, dtype=jnp.int32)
    named = jnp.any(pair_routes[:, :, None] == expert_ids[None, None, :], axis=1)
    extra = 3 * expert_total + 2
    tail = -(width_local + extra) % 128
    content = jnp.concatenate(
        [
            gained.astype(bf16),
            logit_high,
            logit_low,
            named.astype(bf16),
            square_high,
            square_low,
            jnp.zeros((pair_rows, tail), bf16),
        ],
        axis=1,
    )
    pair_slot_count = sections * capacity
    block_of_row = jnp.arange(pair_rows, dtype=jnp.int32)[:, None] // block_rows
    kept = pair_slots < capacity
    slot_index = pair_routes * pair_slot_count + block_of_row * capacity + pair_slots
    slot_index = jnp.where(kept, slot_index, -1)
    slot_ids = jnp.arange(expert_total * pair_slot_count, dtype=jnp.int32)
    placement = jnp.any(slot_index[:, :, None] == slot_ids[None, None, :], axis=1).astype(bf16)
    buffer = jnp.einsum("be,bd->ed", placement, content, preferred_element_type=f32).astype(bf16)
    buffer = buffer.reshape(expert_total, pair_slot_count, content.shape[1])
    received = lax.all_to_all(buffer, "grp", split_axis=0, concat_axis=0, tiled=True)
    received = received.reshape(groups * pair_slot_count, content.shape[1])

    own_slots = received.shape[0] // members
    unit = w_gateup.shape[3]
    gate_up = jnp.dot(
        received[:, :width_local],
        w_gateup[0].reshape(width_local, 2 * unit),
        preferred_element_type=f32,
    ).astype(bf16)
    sums_out = jnp.concatenate(
        [gate_up, received[:, width_local : width_local + extra], jnp.zeros((received.shape[0], 128 - extra), bf16)],
        axis=1,
    ).reshape(members, own_slots, 2 * unit + 128)
    sums_in = lax.all_to_all(sums_out, "dev", split_axis=0, concat_axis=0, tiled=True)
    total = jnp.sum(sums_in.astype(f32), axis=0)
    side = total[:, 2 * unit :]
    logits = side[:, :expert_total] + side[:, expert_total : 2 * expert_total]
    chosen = side[:, 2 * expert_total : 3 * expert_total] > 0.5
    squares = side[:, 3 * expert_total : 3 * expert_total + 1] + side[:, 3 * expert_total + 1 : 3 * expert_total + 2]
    inverse_rms = lax.rsqrt(squares / (width_local * members) + norm_eps)
    sigmoid_scores = jax.nn.sigmoid(logits * inverse_rms)
    own_expert = (expert_ids == lax.axis_index("grp"))[None, :]
    picked = jnp.sum(jnp.where(own_expert, sigmoid_scores, 0.0), axis=-1, keepdims=True)
    denominator = jnp.sum(jnp.where(chosen, sigmoid_scores, 0.0), axis=-1, keepdims=True)
    occupied = jnp.any(chosen, axis=-1, keepdims=True)
    route_weight = jnp.where(occupied, route_scale * picked / jnp.where(occupied, denominator, 1.0), 0.0)
    gate = total[:, :unit] * inverse_rms
    up = total[:, unit : 2 * unit] * inverse_rms
    activated = (jax.nn.silu(gate) * up * route_weight).astype(bf16)

    everyone = spread(activated, "dev").reshape(members * own_slots, unit)
    down = jnp.dot(everyone, w_down[0], preferred_element_type=f32).astype(bf16)
    down = down.reshape(groups, pair_slot_count, width_local)
    returned = lax.all_to_all(down, "grp", split_axis=0, concat_axis=0, tiled=True)
    returned = returned.reshape(expert_total * pair_slot_count, width_local)
    mixture = jnp.dot(placement, returned, preferred_element_type=f32)
    mixture = mixture.reshape(sections, block_rows, width_local)
    both_halves = lax.all_gather(
        lax.dynamic_index_in_dim(mixture, other, 0, False), "sec", axis=0
    )
    from_other = lax.dynamic_index_in_dim(both_halves, other, 0, False)
    mine = lax.dynamic_index_in_dim(mixture, section, 0, False)
    return (hidden_mine + mine + from_other).astype(bf16)


def solution(mesh):
    in_specs = (
        P(("grp", "dev"), None, None),
        P(("grp", "dev"), None),
        P(("grp", "dev"), "sec", None),
        P(("grp", "dev"), None, "sec"),
        P(("grp", "dev")),
        P(("sec", "grp"), None, None),
        P(("sec", "grp"), "dev"),
        P(("sec", "grp"), "dev"),
        P("dev"),
        P("dev", None),
        P(("sec", "grp"), None),
        P(("sec", "grp"), None),
        P("grp", "dev", None, "sec"),
        P("grp", "sec", "dev"),
    )
    out_specs = P(("sec", "grp"), "dev")
    return jax.shard_map(body, mesh=mesh, in_specs=in_specs, out_specs=out_specs, check_vma=False)
```

```python
import functools

import jax
import jax.numpy as jnp
from jax import lax
from jax.experimental import pallas as pl
from jax.experimental.pallas import tpu as pltpu
from jax.sharding import PartitionSpec as P

score_scale = 0.07216878364870323
route_scale = 2.5
norm_eps = 1e-06
masked_floor = -1e30
f32 = jnp.float32
bf16 = jnp.bfloat16


def split_2(value):
    high = value.astype(bf16)
    low = (value - high.astype(f32)).astype(bf16)
    return high, low


def spread(value, axis):
    copies = jnp.broadcast_to(value[None], (lax.axis_size(axis),) + value.shape)
    return lax.all_to_all(copies, axis, split_axis=0, concat_axis=0, tiled=True)


def in_vmem(count):
    return [pl.BlockSpec(memory_space=pltpu.VMEM) for _ in range(count)]


def iota(shape, axis):
    return lax.broadcasted_iota(jnp.int32, shape, axis)


def one_hot(condition):
    return jnp.where(condition, 1.0, 0.0).astype(bf16)


def select_rows(selection, rows):
    return jnp.dot(selection, rows, preferred_element_type=f32).astype(bf16)


def dot_nt(left, right):
    return lax.dot_general(left, right, (((1,), (1,)), ((), ())), preferred_element_type=f32)


def project_kernel(gathered_ref, weight_ref, out_ref):
    members, groups, width = gathered_ref.shape
    total = members * groups
    rows = gathered_ref[...].reshape(total, width)
    target = iota((total, total), 0)
    source = iota((total, total), 1)
    wanted = (target >> 3 & 1) * (total // 2) + (target >> 4) * 8 + (target & 7)
    found = (source & (groups - 1)) * members + (source >> 4)
    rows = select_rows(one_hot(wanted == found), rows)
    out = dot_nt(rows, weight_ref[...]).astype(bf16)
    out_ref[...] = out.reshape(out_ref.shape)


def gate_up_kernel(received_ref, weight_ref, out_ref):
    members, chunk, width = received_ref.shape
    total = members * chunk
    rows = received_ref[...].reshape(total, width)
    shape = (24 * members, total)
    target = iota(shape, 0)
    source = iota(shape, 1)
    base = 24 * (source >> 4)
    slot = source & 15
    gate_rows = select_rows(one_hot((target == base + slot) & (slot < 12)), rows)
    place = base + jnp.where(slot < 8, slot + 16, slot + 4)
    up_rows = select_rows(one_hot((target == place) & (slot < 12)), rows)
    left = jnp.concatenate([gate_rows, up_rows], axis=1)
    sums = jnp.dot(left, weight_ref[...], preferred_element_type=f32)
    side = received_ref[:, :, width - 128 :].astype(f32)
    first = iota((8, 128), 1) < 64
    columns = sums.shape[1] // 128
    for member in range(members):
        tiles = [
            sums[24 * member + 8 * row : 24 * member + 8 * row + 8, 128 * col : 128 * col + 128]
            for row in range(3)
            for col in range(columns)
        ]
        turned = pltpu.roll(side[member, :8], 64, 1)
        tiles.append(jnp.where(first, turned, side[member, 8:]))
        out_ref[member] = jnp.concatenate(tiles, axis=0).astype(bf16)


def activate_kernel(model_width, expert_total, sums_ref, expert_ref, out_ref):
    members, height, _ = sums_ref.shape
    columns = height // 24
    total = sums_ref[0].astype(f32)
    for member in range(1, members):
        total = total + sums_ref[member].astype(f32)

    def block(row):
        first = 8 * columns * row
        return jnp.concatenate(
            [total[first + 8 * col : first + 8 * col + 8] for col in range(columns)], axis=1
        )

    side = total[24 * columns :]
    side = jnp.concatenate([side, pltpu.roll(side, 64, 1)], axis=0)
    lane = iota(side.shape, 1)
    logits = side + pltpu.roll(side, 128 - expert_total, 1)
    named = pltpu.roll(side, 128 - 2 * expert_total, 1)
    square_lane = 3 * expert_total
    is_square = (lane == square_lane) | (lane == square_lane + 1)
    squares = jnp.sum(jnp.where(is_square, side, 0.0), axis=1, keepdims=True)
    inverse_rms = lax.rsqrt(squares / model_width + norm_eps)
    scores = 1.0 / (1.0 + jnp.exp(-jnp.where(lane < expert_total, logits * inverse_rms, 0.0)))
    chosen = (named > 0.5) & (lane < expert_total)
    picked = jnp.sum(jnp.where(lane == expert_ref[0], scores, 0.0), axis=1, keepdims=True)
    denominator = jnp.sum(jnp.where(chosen, scores, 0.0), axis=1, keepdims=True)
    occupied = denominator > 0.0
    weight = route_scale * picked / jnp.where(occupied, denominator, 1.0)
    weight = jnp.where(occupied, weight, 0.0)

    def activation(gate, up, scale, share):
        gate = gate * scale
        return gate / (1.0 + jnp.exp(-gate)) * (up * scale) * share

    early = activation(block(0), block(2), inverse_rms[:8], weight[:8])
    mixed = block(1)
    late = activation(mixed, pltpu.roll(mixed, 4, 0), inverse_rms[8:], weight[8:])
    half = early.shape[1] // 2
    last = jnp.where(
        iota((8, half), 0) < 4, late[:, :half], pltpu.roll(late[:, half:], 4, 0)
    )
    packed = jnp.concatenate([early[:, :half], early[:, half:], last], axis=0).astype(bf16)
    for member in range(out_ref.shape[0]):
        out_ref[member] = packed


def down_kernel(packed_ref, weight_ref, out_ref):
    members, height, half = packed_ref.shape
    rows = packed_ref[...].reshape(members * height, half)
    shape = (16 * members, members * height)
    target = iota(shape, 0)
    source = iota(shape, 1)
    base = 24 * (target >> 4)
    slot = target & 15
    low_place = base + jnp.where(slot < 8, slot, slot + 8)
    high_place = base + jnp.where(slot < 8, slot + 8, slot + 12)
    low = select_rows(one_hot((source == low_place) & (slot < 12)), rows)
    high = select_rows(one_hot((source == high_place) & (slot < 12)), rows)
    out = dot_nt(jnp.concatenate([low, high], axis=1), weight_ref[...]).astype(bf16)
    out_ref[...] = out.reshape(out_ref.shape)


def body(
    q_latent,
    q_rope,
    cache_latent,
    cache_rope,
    lengths,
    w_uv,
    w_out,
    resid,
    norm_gain,
    router,
    routes,
    slots,
    w_gateup,
    w_down,
):
    sections = lax.axis_size("sec")
    groups = lax.axis_size("grp")
    members = lax.axis_size("dev")
    section = lax.axis_index("sec")
    _, head_total, latent = q_latent.shape
    hist_local = cache_latent.shape[1]
    rope_width = cache_rope.shape[1]
    half_heads = head_total // sections
    head_block, _, value_width = w_uv.shape
    block_rows, width_local = resid.shape
    choices = routes.shape[1]
    expert_total = router.shape[1]
    capacity = max(2, 3 * block_rows // 4)
    pair_rows = sections * block_rows
    vmem = pltpu.CompilerParams(vmem_limit_bytes=32 * 2**20)

    query = q_latent[0]
    rope_query = q_rope.reshape(head_total, rope_width)
    scores = (
        jnp.einsum("hc,pc->hp", query, cache_latent[0], preferred_element_type=f32)
        + jnp.einsum("hj,jp->hp", rope_query, cache_rope[0], preferred_element_type=f32)
    ) * score_scale
    positions = section * hist_local + jnp.arange(hist_local, dtype=jnp.int32)
    usable = (positions < lengths[0])[None, :]
    masked = jnp.where(usable, scores, masked_floor)
    top = jnp.max(masked, axis=-1, keepdims=True).astype(bf16)
    expon = jnp.where(usable, jnp.exp(masked - top.astype(f32)), 0.0)
    mass = jnp.sum(expon, axis=-1, keepdims=True)
    weighted = jnp.dot(expon.astype(bf16), cache_latent[0], preferred_element_type=f32)

    mass_high, mass_low = split_2(mass)
    route_part = jnp.concatenate([routes, slots], axis=1).astype(bf16)
    route_part = jnp.pad(route_part, ((0, half_heads - block_rows), (0, 0)))

    def half(value, which):
        return lax.dynamic_slice_in_dim(value, which * half_heads, half_heads, 0)

    other = 1 - section
    spare = 128 - 3 - 2 * choices
    outgoing = jnp.concatenate(
        [
            half(weighted, other).astype(bf16),
            half(top, other),
            half(mass_high, other),
            half(mass_low, other),
            route_part,
            jnp.zeros((half_heads, spare), bf16),
        ],
        axis=1,
    )
    both = lax.all_gather(outgoing, "sec", axis=0)
    theirs = lax.dynamic_index_in_dim(both, other, 0, False)
    top_mine = half(top, section).astype(f32)
    top_theirs = theirs[:, latent : latent + 1].astype(f32)
    mass_theirs = (
        theirs[:, latent + 1 : latent + 2].astype(f32)
        + theirs[:, latent + 2 : latent + 3].astype(f32)
    )
    top_both = jnp.maximum(top_mine, top_theirs)
    factor_mine = jnp.exp(top_mine - top_both)
    factor_theirs = jnp.exp(top_theirs - top_both)
    mass_both = half(mass, section) * factor_mine + mass_theirs * factor_theirs
    latent_out = (
        half(weighted, section) * factor_mine + theirs[:, :latent].astype(f32) * factor_theirs
    ) / mass_both
    latent_out = latent_out.astype(bf16)
    pair_table = both[:, :block_rows, latent + 3 : latent + 3 + 2 * choices]
    pair_table = pair_table.reshape(pair_rows, 2 * choices).astype(jnp.int32)
    pair_routes, pair_slots = pair_table[:, :choices], pair_table[:, choices:]

    outgoing_heads = latent_out.reshape(groups, head_block, latent)
    arrived = lax.all_to_all(outgoing_heads, "grp", split_axis=0, concat_axis=0, tiled=True)
    values = jnp.einsum("nhc,hcv->nhv", arrived, w_uv, preferred_element_type=f32).astype(bf16)
    width_heads = head_block * value_width
    gathered = spread(values.reshape(groups, width_heads), "dev")
    partial = pl.pallas_call(
        project_kernel,
        out_shape=jax.ShapeDtypeStruct((groups, pair_rows, width_local), bf16),
        in_specs=in_vmem(2),
        out_specs=in_vmem(1)[0],
        compiler_params=vmem,
    )(gathered, w_out.T)
    partial = lax.all_to_all(partial, "grp", split_axis=0, concat_axis=0, tiled=True)
    summed = jnp.sum(partial.astype(f32), axis=0).reshape(sections, block_rows, width_local)
    is_mine = (jnp.arange(sections) == section)[:, None, None]
    summed = summed + jnp.where(is_mine, resid.astype(f32)[None], 0.0)
    hidden = jnp.sum(lax.all_gather(summed, "sec", axis=0), axis=0)
    hidden_mine = lax.dynamic_index_in_dim(hidden, section, 0, False)
    hidden = hidden.reshape(pair_rows, width_local)

    gained = hidden * norm_gain
    square_high, square_low = split_2(jnp.sum(hidden * hidden, axis=-1, keepdims=True))
    logit_high, logit_low = split_2(jnp.dot(gained, router, precision=lax.Precision.HIGHEST))
    expert_ids = jnp.arange(expert_total, dtype=jnp.int32)
    named = jnp.any(pair_routes[:, :, None] == expert_ids[None, None, :], axis=1)
    extra = 3 * expert_total + 2
    tail = -(width_local + extra) % 128
    content = jnp.concatenate(
        [
            gained.astype(bf16),
            logit_high,
            logit_low,
            named.astype(bf16),
            square_high,
            square_low,
            jnp.zeros((pair_rows, tail), bf16),
        ],
        axis=1,
    )
    chunk = 16
    block_of_row = jnp.arange(pair_rows, dtype=jnp.int32)[:, None] // block_rows
    kept = pair_slots < capacity
    slot_index = pair_routes * chunk + block_of_row * capacity + pair_slots
    slot_index = jnp.where(kept, slot_index, -1)
    slot_ids = jnp.arange(expert_total * chunk, dtype=jnp.int32)
    placement = jnp.any(slot_index[:, :, None] == slot_ids[None, None, :], axis=1).astype(bf16)
    buffer = jnp.einsum("be,bd->ed", placement, content, preferred_element_type=f32).astype(bf16)
    buffer = buffer.reshape(expert_total, chunk, content.shape[1])
    received = lax.all_to_all(buffer, "grp", split_axis=0, concat_axis=0, tiled=True)

    unit = w_gateup.shape[3]
    weight = jnp.pad(
        w_gateup[0].transpose(1, 0, 2), ((0, 0), (0, content.shape[1] - width_local), (0, 0))
    ).reshape(2 * content.shape[1], unit)
    sums = pl.pallas_call(
        gate_up_kernel,
        out_shape=jax.ShapeDtypeStruct((members, 24 * unit // 128 + 8, 128), bf16),
        in_specs=in_vmem(2),
        out_specs=in_vmem(1)[0],
        compiler_params=vmem,
    )(received, weight)
    sums = lax.all_to_all(sums, "dev", split_axis=0, concat_axis=0, tiled=True)
    packed = pl.pallas_call(
        functools.partial(activate_kernel, width_local * members, expert_total),
        out_shape=jax.ShapeDtypeStruct((members, 24, unit // 2), bf16),
        in_specs=[in_vmem(1)[0], pl.BlockSpec(memory_space=pltpu.SMEM)],
        out_specs=in_vmem(1)[0],
        compiler_params=vmem,
    )(sums, lax.axis_index("grp").reshape(1))

    everyone = lax.all_to_all(packed, "dev", split_axis=0, concat_axis=0, tiled=True)
    down = pl.pallas_call(
        down_kernel,
        out_shape=jax.ShapeDtypeStruct((groups, chunk, width_local), bf16),
        in_specs=in_vmem(2),
        out_specs=in_vmem(1)[0],
        compiler_params=vmem,
    )(everyone, w_down[0].T)
    returned = lax.all_to_all(down, "grp", split_axis=0, concat_axis=0, tiled=True)
    returned = returned.reshape(expert_total * chunk, width_local)
    mixture = jnp.dot(placement, returned, preferred_element_type=f32)
    mixture = mixture.reshape(sections, block_rows, width_local)
    both_halves = lax.all_gather(
        lax.dynamic_index_in_dim(mixture, other, 0, False), "sec", axis=0
    )
    from_other = lax.dynamic_index_in_dim(both_halves, other, 0, False)
    mine = lax.dynamic_index_in_dim(mixture, section, 0, False)
    return (hidden_mine + mine + from_other).astype(bf16)


def solution(mesh):
    in_specs = (
        P(("grp", "dev"), None, None),
        P(("grp", "dev"), None),
        P(("grp", "dev"), "sec", None),
        P(("grp", "dev"), None, "sec"),
        P(("grp", "dev")),
        P(("sec", "grp"), None, None),
        P(("sec", "grp"), "dev"),
        P(("sec", "grp"), "dev"),
        P("dev"),
        P("dev", None),
        P(("sec", "grp"), None),
        P(("sec", "grp"), None),
        P("grp", "dev", None, "sec"),
        P("grp", "sec", "dev"),
    )
    out_specs = P(("sec", "grp"), "dev")
    return jax.shard_map(body, mesh=mesh, in_specs=in_specs, out_specs=out_specs, check_vma=False)
```

```python
import functools

import jax
import jax.numpy as jnp
from jax import lax
from jax.experimental import pallas as pl
from jax.experimental.pallas import tpu as pltpu
from jax.sharding import PartitionSpec as P

score_scale = 0.07216878364870323
route_scale = 2.5
norm_eps = 1e-06
masked_floor = -1e30
f32 = jnp.float32
bf16 = jnp.bfloat16


def spread(value, axis):
    copies = jnp.broadcast_to(value[None], (lax.axis_size(axis),) + value.shape)
    return lax.all_to_all(copies, axis, split_axis=0, concat_axis=0, tiled=True)


def in_vmem(count):
    return [pl.BlockSpec(memory_space=pltpu.VMEM) for _ in range(count)]


def iota(shape, axis):
    return lax.broadcasted_iota(jnp.int32, shape, axis)


def one_hot(condition):
    return jnp.where(condition, 1.0, 0.0).astype(bf16)


def select_rows(selection, rows):
    return jnp.dot(selection, rows, preferred_element_type=f32).astype(bf16)


def dot_nt(left, right):
    return lax.dot_general(left, right, (((1,), (1,)), ((), ())), preferred_element_type=f32)


def attend_kernel(
    place_ref, latent_ref, rope_ref, cache_ref, cache_rope_ref, routes_ref, slots_ref, sent_ref, kept_ref
):
    heads = latent_ref.shape[0]
    half = heads // 2
    latent = latent_ref.shape[1]
    mine = pl.multiple_of(place_ref[0] * half, half)
    other = pl.multiple_of(half - place_ref[0] * half, half)

    def other_first(ref):
        return jnp.concatenate([ref[pl.ds(other, half), :], ref[pl.ds(mine, half), :]], axis=0)

    cache = cache_ref[...]
    scores = dot_nt(other_first(latent_ref), cache) + jnp.dot(
        other_first(rope_ref), cache_rope_ref[...], preferred_element_type=f32
    )
    usable = iota(scores.shape, 1) < place_ref[1]
    masked = jnp.where(usable, scores * score_scale, masked_floor)
    top = jnp.max(masked, axis=1, keepdims=True).astype(bf16).astype(f32)
    expon = jnp.where(usable, jnp.exp(masked - top), 0.0)
    mass = jnp.sum(expon, axis=1, keepdims=True)
    weighted = jnp.dot(expon.astype(bf16), cache, preferred_element_type=f32)
    mass_high = mass.astype(bf16).astype(f32)
    lane = iota((heads, 128), 1)
    side = jnp.where(lane == 0, top, 0.0)
    side = jnp.where(lane == 1, mass_high, side)
    side = jnp.where(lane == 2, mass - mass_high, side)
    kept_ref[:, :latent] = weighted[half:]
    kept_ref[:, latent:] = side[half:]
    choices = routes_ref.shape[1]
    spot = iota((choices, 128), 1) - iota((choices, 128), 0)
    table = jnp.dot(
        routes_ref[...].astype(f32), jnp.where(spot == 16, 1.0, 0.0), preferred_element_type=f32
    ) + jnp.dot(
        slots_ref[...].astype(f32), jnp.where(spot == 16 + choices, 1.0, 0.0), preferred_element_type=f32
    )
    block_rows = table.shape[0]
    side = jnp.concatenate([side[:block_rows] + table, side[block_rows:half]], axis=0)
    sent_ref[:, :latent] = weighted[:half].astype(bf16)
    sent_ref[:, latent:] = side.astype(bf16)


def dispatch_kernel(
    expert_total, sums_ref, gain_ref, router_ref, named_ref, placement_ref, buffer_ref, hidden_ref
):
    hidden = sums_ref[0] + sums_ref[1]
    hidden_ref[...] = hidden
    rows, width = hidden.shape
    gained = hidden * gain_ref[...]
    squares = jnp.sum(hidden * hidden, axis=1, keepdims=True)
    square_high = squares.astype(bf16).astype(f32)
    logits = lax.dot_general(
        gained,
        router_ref[...],
        (((1,), (1,)), ((), ())),
        preferred_element_type=f32,
        precision=lax.Precision.HIGHEST,
    )
    spread_out = jnp.concatenate([logits, jnp.zeros((rows, 128 - expert_total), f32)], axis=1)
    logit_high = spread_out.astype(bf16).astype(f32)
    lane = iota((rows, 128), 1)
    first = width % 128
    side = pltpu.roll(logit_high, first, 1) + pltpu.roll(
        spread_out - logit_high, first + expert_total, 1
    )
    side = side + pltpu.roll(named_ref[...], first + 2 * expert_total, 1)
    side = jnp.where(lane == first + 3 * expert_total, square_high, side)
    side = jnp.where(lane == first + 3 * expert_total + 1, squares - square_high, side)
    full = width - first
    last = jnp.concatenate([gained[:, full:], jnp.zeros((rows, 128 - first), f32)], axis=1)
    content = jnp.concatenate([gained[:, :full], jnp.where(lane < first, last, side)], axis=1)
    out = jnp.dot(placement_ref[...], content.astype(bf16), preferred_element_type=f32)
    buffer_ref[...] = out.astype(bf16).reshape(buffer_ref.shape)


def project_kernel(gathered_ref, weight_ref, out_ref):
    members, groups, width = gathered_ref.shape
    total = members * groups
    rows = gathered_ref[...].reshape(total, width)
    target = iota((total, total), 0)
    source = iota((total, total), 1)
    wanted = (target >> 3 & 1) * (total // 2) + (target >> 4) * 8 + (target & 7)
    found = (source & (groups - 1)) * members + (source >> 4)
    rows = select_rows(one_hot(wanted == found), rows)
    out = dot_nt(rows, weight_ref[...]).astype(bf16)
    out_ref[...] = out.reshape(out_ref.shape)


def gate_up_kernel(received_ref, weight_ref, out_ref):
    members, chunk, width = received_ref.shape
    total = members * chunk
    rows = received_ref[...].reshape(total, width)
    shape = (24 * members, total)
    target = iota(shape, 0)
    source = iota(shape, 1)
    base = 24 * (source >> 4)
    slot = source & 15
    gate_rows = select_rows(one_hot((target == base + slot) & (slot < 12)), rows)
    place = base + jnp.where(slot < 8, slot + 16, slot + 4)
    up_rows = select_rows(one_hot((target == place) & (slot < 12)), rows)
    left = jnp.concatenate([gate_rows, up_rows], axis=1)
    sums = jnp.dot(left, weight_ref[...], preferred_element_type=f32)
    side = received_ref[:, :, width - 128 :].astype(f32)
    first = iota((8, 128), 1) < 64
    columns = sums.shape[1] // 128
    for member in range(members):
        tiles = [
            sums[24 * member + 8 * row : 24 * member + 8 * row + 8, 128 * col : 128 * col + 128]
            for row in range(3)
            for col in range(columns)
        ]
        turned = pltpu.roll(side[member, :8], 64, 1)
        tiles.append(jnp.where(first, turned, side[member, 8:]))
        out_ref[member] = jnp.concatenate(tiles, axis=0).astype(bf16)


def activate_kernel(model_width, expert_total, sums_ref, expert_ref, out_ref):
    members, height, _ = sums_ref.shape
    columns = height // 24
    total = sums_ref[0].astype(f32)
    for member in range(1, members):
        total = total + sums_ref[member].astype(f32)

    def block(row):
        first = 8 * columns * row
        return jnp.concatenate(
            [total[first + 8 * col : first + 8 * col + 8] for col in range(columns)], axis=1
        )

    side = total[24 * columns :]
    side = jnp.concatenate([side, pltpu.roll(side, 64, 1)], axis=0)
    lane = iota(side.shape, 1)
    logits = side + pltpu.roll(side, 128 - expert_total, 1)
    named = pltpu.roll(side, 128 - 2 * expert_total, 1)
    square_lane = 3 * expert_total
    is_square = (lane == square_lane) | (lane == square_lane + 1)
    squares = jnp.sum(jnp.where(is_square, side, 0.0), axis=1, keepdims=True)
    inverse_rms = lax.rsqrt(squares / model_width + norm_eps)
    scores = 1.0 / (1.0 + jnp.exp(-jnp.where(lane < expert_total, logits * inverse_rms, 0.0)))
    chosen = (named > 0.5) & (lane < expert_total)
    picked = jnp.sum(jnp.where(lane == expert_ref[0], scores, 0.0), axis=1, keepdims=True)
    denominator = jnp.sum(jnp.where(chosen, scores, 0.0), axis=1, keepdims=True)
    occupied = denominator > 0.0
    weight = route_scale * picked / jnp.where(occupied, denominator, 1.0)
    weight = jnp.where(occupied, weight, 0.0)

    def activation(gate, up, scale, share):
        gate = gate * scale
        return gate / (1.0 + jnp.exp(-gate)) * (up * scale) * share

    early = activation(block(0), block(2), inverse_rms[:8], weight[:8])
    mixed = block(1)
    late = activation(mixed, pltpu.roll(mixed, 4, 0), inverse_rms[8:], weight[8:])
    half = early.shape[1] // 2
    last = jnp.where(
        iota((8, half), 0) < 4, late[:, :half], pltpu.roll(late[:, half:], 4, 0)
    )
    packed = jnp.concatenate([early[:, :half], early[:, half:], last], axis=0).astype(bf16)
    for member in range(out_ref.shape[0]):
        out_ref[member] = packed


def down_kernel(packed_ref, weight_ref, out_ref):
    members, height, half = packed_ref.shape
    rows = packed_ref[...].reshape(members * height, half)
    shape = (16 * members, members * height)
    target = iota(shape, 0)
    source = iota(shape, 1)
    base = 24 * (target >> 4)
    slot = target & 15
    low_place = base + jnp.where(slot < 8, slot, slot + 8)
    high_place = base + jnp.where(slot < 8, slot + 8, slot + 12)
    low = select_rows(one_hot((source == low_place) & (slot < 12)), rows)
    high = select_rows(one_hot((source == high_place) & (slot < 12)), rows)
    out = dot_nt(jnp.concatenate([low, high], axis=1), weight_ref[...]).astype(bf16)
    out_ref[...] = out.reshape(out_ref.shape)


def body(
    q_latent,
    q_rope,
    cache_latent,
    cache_rope,
    lengths,
    w_uv,
    w_out,
    resid,
    norm_gain,
    router,
    routes,
    slots,
    w_gateup,
    w_down,
):
    sections = lax.axis_size("sec")
    groups = lax.axis_size("grp")
    members = lax.axis_size("dev")
    section = lax.axis_index("sec")
    _, head_total, latent = q_latent.shape
    hist_local = cache_latent.shape[1]
    rope_width = cache_rope.shape[1]
    half_heads = head_total // sections
    head_block, _, value_width = w_uv.shape
    block_rows, width_local = resid.shape
    choices = routes.shape[1]
    expert_total = router.shape[1]
    capacity = max(2, 3 * block_rows // 4)
    pair_rows = sections * block_rows
    vmem = pltpu.CompilerParams(vmem_limit_bytes=32 * 2**20)

    place = jnp.stack([section, lengths[0] - section * hist_local]).astype(jnp.int32)
    sent, kept_part = pl.pallas_call(
        attend_kernel,
        out_shape=(
            jax.ShapeDtypeStruct((half_heads, latent + 128), bf16),
            jax.ShapeDtypeStruct((half_heads, latent + 128), f32),
        ),
        in_specs=[pl.BlockSpec(memory_space=pltpu.SMEM)] + in_vmem(6),
        out_specs=tuple(in_vmem(2)),
        compiler_params=vmem,
    )(
        place,
        q_latent[0],
        q_rope.reshape(head_total, rope_width),
        cache_latent[0],
        cache_rope[0],
        routes,
        slots,
    )

    other = 1 - section
    both = lax.all_gather(sent, "sec", axis=0)
    theirs = lax.dynamic_index_in_dim(both, other, 0, False)
    top_mine = kept_part[:, latent : latent + 1]
    mass_mine = kept_part[:, latent + 1 : latent + 2] + kept_part[:, latent + 2 : latent + 3]
    top_theirs = theirs[:, latent : latent + 1].astype(f32)
    mass_theirs = (
        theirs[:, latent + 1 : latent + 2].astype(f32)
        + theirs[:, latent + 2 : latent + 3].astype(f32)
    )
    top_both = jnp.maximum(top_mine, top_theirs)
    factor_mine = jnp.exp(top_mine - top_both)
    factor_theirs = jnp.exp(top_theirs - top_both)
    mass_both = mass_mine * factor_mine + mass_theirs * factor_theirs
    latent_out = (
        kept_part[:, :latent] * factor_mine + theirs[:, :latent].astype(f32) * factor_theirs
    ) / mass_both
    latent_out = latent_out.astype(bf16)
    pair_table = both[:, :block_rows, latent + 16 : latent + 16 + 2 * choices]
    pair_table = pair_table.reshape(pair_rows, 2 * choices).astype(jnp.int32)
    pair_routes, pair_slots = pair_table[:, :choices], pair_table[:, choices:]

    outgoing_heads = latent_out.reshape(groups, head_block, latent)
    arrived = lax.all_to_all(outgoing_heads, "grp", split_axis=0, concat_axis=0, tiled=True)
    values = jnp.einsum("nhc,hcv->nhv", arrived, w_uv, preferred_element_type=f32).astype(bf16)
    width_heads = head_block * value_width
    gathered = spread(values.reshape(groups, width_heads), "dev")
    partial = pl.pallas_call(
        project_kernel,
        out_shape=jax.ShapeDtypeStruct((groups, pair_rows, width_local), bf16),
        in_specs=in_vmem(2),
        out_specs=in_vmem(1)[0],
        compiler_params=vmem,
    )(gathered, w_out.T)
    partial = lax.all_to_all(partial, "grp", split_axis=0, concat_axis=0, tiled=True)
    summed = jnp.sum(partial.astype(f32), axis=0).reshape(sections, block_rows, width_local)
    is_mine = (jnp.arange(sections) == section)[:, None, None]
    summed = summed + jnp.where(is_mine, resid.astype(f32)[None], 0.0)
    summed = lax.all_gather(summed.reshape(pair_rows, width_local), "sec", axis=0)

    expert_ids = jnp.arange(expert_total, dtype=jnp.int32)
    named = jnp.any(pair_routes[:, :, None] == expert_ids[None, None, :], axis=1)
    named = jnp.pad(named.astype(f32), ((0, 0), (0, 128 - expert_total)))
    chunk = 16
    block_of_row = jnp.arange(pair_rows, dtype=jnp.int32)[:, None] // block_rows
    kept = pair_slots < capacity
    slot_index = pair_routes * chunk + block_of_row * capacity + pair_slots
    slot_index = jnp.where(kept, slot_index, -1)
    slot_ids = jnp.arange(expert_total * chunk, dtype=jnp.int32)
    placement = jnp.any(slot_index[:, :, None] == slot_ids[None, None, :], axis=1).astype(bf16)
    padded_width = width_local + -width_local % 128
    buffer, hidden = pl.pallas_call(
        functools.partial(dispatch_kernel, expert_total),
        out_shape=(
            jax.ShapeDtypeStruct((expert_total, chunk, padded_width), bf16),
            jax.ShapeDtypeStruct((pair_rows, width_local), f32),
        ),
        in_specs=in_vmem(5),
        out_specs=tuple(in_vmem(2)),
        compiler_params=vmem,
    )(summed, norm_gain[None], router.T, named, placement.T)
    received = lax.all_to_all(buffer, "grp", split_axis=0, concat_axis=0, tiled=True)

    unit = w_gateup.shape[3]
    weight = jnp.pad(
        w_gateup[0].transpose(1, 0, 2), ((0, 0), (0, padded_width - width_local), (0, 0))
    ).reshape(2 * padded_width, unit)
    sums = pl.pallas_call(
        gate_up_kernel,
        out_shape=jax.ShapeDtypeStruct((members, 24 * unit // 128 + 8, 128), bf16),
        in_specs=in_vmem(2),
        out_specs=in_vmem(1)[0],
        compiler_params=vmem,
    )(received, weight)
    sums = lax.all_to_all(sums, "dev", split_axis=0, concat_axis=0, tiled=True)
    packed = pl.pallas_call(
        functools.partial(activate_kernel, width_local * members, expert_total),
        out_shape=jax.ShapeDtypeStruct((members, 24, unit // 2), bf16),
        in_specs=[in_vmem(1)[0], pl.BlockSpec(memory_space=pltpu.SMEM)],
        out_specs=in_vmem(1)[0],
        compiler_params=vmem,
    )(sums, lax.axis_index("grp").reshape(1))

    everyone = lax.all_to_all(packed, "dev", split_axis=0, concat_axis=0, tiled=True)
    down = pl.pallas_call(
        down_kernel,
        out_shape=jax.ShapeDtypeStruct((groups, chunk, width_local), bf16),
        in_specs=in_vmem(2),
        out_specs=in_vmem(1)[0],
        compiler_params=vmem,
    )(everyone, w_down[0].T)
    returned = lax.all_to_all(down, "grp", split_axis=0, concat_axis=0, tiled=True)
    returned = returned.reshape(expert_total * chunk, width_local)
    mixture = jnp.dot(placement, returned, preferred_element_type=f32)
    mixture = mixture.reshape(sections, block_rows, width_local)
    both_halves = lax.all_gather(
        lax.dynamic_index_in_dim(mixture, other, 0, False), "sec", axis=0
    )
    from_other = lax.dynamic_index_in_dim(both_halves, other, 0, False)
    mine = lax.dynamic_index_in_dim(mixture, section, 0, False)
    hidden_mine = lax.dynamic_slice_in_dim(hidden, section * block_rows, block_rows, 0)
    return (hidden_mine + mine + from_other).astype(bf16)


def solution(mesh):
    in_specs = (
        P(("grp", "dev"), None, None),
        P(("grp", "dev"), None),
        P(("grp", "dev"), "sec", None),
        P(("grp", "dev"), None, "sec"),
        P(("grp", "dev")),
        P(("sec", "grp"), None, None),
        P(("sec", "grp"), "dev"),
        P(("sec", "grp"), "dev"),
        P("dev"),
        P("dev", None),
        P(("sec", "grp"), None),
        P(("sec", "grp"), None),
        P("grp", "dev", None, "sec"),
        P("grp", "sec", "dev"),
    )
    out_specs = P(("sec", "grp"), "dev")
    return jax.shard_map(body, mesh=mesh, in_specs=in_specs, out_specs=out_specs, check_vma=False)
```

```python
import functools

import jax
import jax.numpy as jnp
from jax import lax
from jax.experimental import pallas as pl
from jax.experimental.pallas import tpu as pltpu
from jax.sharding import PartitionSpec as P

score_scale = 0.07216878364870323
route_scale = 2.5
norm_eps = 1e-06
masked_floor = -1e30
f32 = jnp.float32
bf16 = jnp.bfloat16


def spread(value, axis):
    copies = jnp.broadcast_to(value[None], (lax.axis_size(axis),) + value.shape)
    return lax.all_to_all(copies, axis, split_axis=0, concat_axis=0, tiled=True)


def in_vmem(count):
    return [pl.BlockSpec(memory_space=pltpu.VMEM) for _ in range(count)]


def iota(shape, axis):
    return lax.broadcasted_iota(jnp.int32, shape, axis)


def one_hot(condition):
    return jnp.where(condition, 1.0, 0.0).astype(bf16)


def select_rows(selection, rows):
    return jnp.dot(selection, rows, preferred_element_type=f32).astype(bf16)


def dot_nt(left, right):
    return lax.dot_general(left, right, (((1,), (1,)), ((), ())), preferred_element_type=f32)


def attend_kernel(
    place_ref,
    latent_hbm,
    rope_hbm,
    cache_hbm,
    cache_rope_hbm,
    routes_ref,
    slots_ref,
    sent_ref,
    kept_ref,
    latent_ref,
    rope_ref,
    cache_ref,
    cache_rope_ref,
    sems,
):
    copies = [
        pltpu.make_async_copy(source, target, sems.at[index])
        for index, (source, target) in enumerate(
            [
                (rope_hbm, rope_ref),
                (cache_rope_hbm, cache_rope_ref),
                (latent_hbm, latent_ref),
                (cache_hbm, cache_ref),
            ]
        )
    ]
    for copy in copies:
        copy.start()
    heads, latent = latent_ref.shape
    half = heads // 2
    width = cache_rope_ref.shape[0]
    mine = pl.multiple_of(place_ref[0] * half, half)
    other = pl.multiple_of(half - place_ref[0] * half, half)

    choices = routes_ref.shape[1]
    spot = iota((choices, 128), 1) - iota((choices, 128), 0)
    table = jnp.dot(
        routes_ref[...].astype(f32), jnp.where(spot == 16, 1.0, 0.0), preferred_element_type=f32
    ) + jnp.dot(
        slots_ref[...].astype(f32), jnp.where(spot == 16 + choices, 1.0, 0.0), preferred_element_type=f32
    )

    copies[0].wait()
    row = rope_ref[...].astype(f32)
    pairs = jnp.concatenate(
        [row[:, 128 * pair : 128 * pair + 128] for pair in range(heads * width // 128)], axis=0
    )
    head = iota((heads, heads // 2), 0) + jnp.where(
        iota((heads, heads // 2), 0) < half, other, mine - half
    )
    picked = select_rows(one_hot(head >> 1 == iota((heads, heads // 2), 1)), pairs.astype(bf16))
    lane_half = iota((heads, 128), 1) >> 6
    picked = jnp.where(lane_half == (iota((heads, 128), 0) & 1), picked, jnp.zeros_like(picked))
    copies[1].wait()
    keys = cache_rope_ref[...]
    rope_scores = jnp.dot(
        picked, jnp.concatenate([keys, keys], axis=0), preferred_element_type=f32
    )
    copies[2].wait()
    query = jnp.concatenate([latent_ref[pl.ds(other, half), :], latent_ref[pl.ds(mine, half), :]], axis=0)
    copies[3].wait()
    cache = cache_ref[...]
    scores = dot_nt(query, cache) + rope_scores
    usable = iota(scores.shape, 1) < place_ref[1]
    masked = jnp.where(usable, scores * score_scale, masked_floor)
    top = jnp.max(masked, axis=1, keepdims=True).astype(bf16).astype(f32)
    expon = jnp.where(usable, jnp.exp(masked - top), 0.0)
    mass = jnp.sum(expon, axis=1, keepdims=True)
    weighted = jnp.dot(expon.astype(bf16), cache, preferred_element_type=f32)
    mass_high = mass.astype(bf16).astype(f32)
    lane = iota((heads, 128), 1)
    side = jnp.where(lane == 0, top, 0.0)
    side = jnp.where(lane == 1, mass_high, side)
    side = jnp.where(lane == 2, mass - mass_high, side)
    kept_ref[:, :latent] = weighted[half:]
    kept_ref[:, latent:] = side[half:]
    block_rows = table.shape[0]
    side = jnp.concatenate([side[:block_rows] + table, side[block_rows:half]], axis=0)
    sent_ref[:, :latent] = weighted[:half].astype(bf16)
    sent_ref[:, latent:] = side.astype(bf16)


def block_sum_kernel(place_ref, partial_ref, resid_ref, out_ref):
    total = partial_ref[0].astype(f32)
    for group in range(1, partial_ref.shape[0]):
        total = total + partial_ref[group].astype(f32)
    block_rows = resid_ref.shape[0]
    resid = resid_ref[...].astype(f32)
    resid = jnp.concatenate([resid] * (total.shape[0] // block_rows), axis=0)
    own = iota(total.shape, 0) // block_rows == place_ref[0]
    out_ref[...] = total + jnp.where(own, resid, 0.0)


def last_sum_kernel(place_ref, halves_ref, hidden_ref, out_ref):
    block_rows = out_ref.shape[0]
    own = pl.ds(pl.multiple_of(place_ref[0] * block_rows, block_rows), block_rows)
    total = hidden_ref[own, :] + halves_ref[0, own, :] + halves_ref[1, own, :]
    out_ref[...] = total.astype(bf16)


def dispatch_kernel(
    expert_total, choices, capacity, sums_ref, gain_ref, router_ref, table_ref, buffer_ref, hidden_ref, placement_ref
):
    table = table_ref[...].astype(f32).reshape(-1, 128)
    rows = table.shape[0]
    chunk = buffer_ref.shape[1]
    slot_total = expert_total * chunk
    lane = iota((rows, 128), 1)
    block = jnp.where(iota((rows, 1), 0) < rows // 2, 0.0, 1.0 * capacity)
    named = jnp.zeros((rows, 128), f32)
    placement = jnp.zeros((rows, slot_total), f32)
    spot = iota((rows, slot_total), 1).astype(f32)
    for choice in range(choices):
        route = table[:, 16 + choice : 17 + choice]
        slot = table[:, 16 + choices + choice : 17 + choices + choice]
        named = jnp.where(lane.astype(f32) == route, 1.0, named)
        filled = jnp.where(slot < capacity, route * chunk + block + slot, -1.0)
        placement = jnp.where(spot == filled, 1.0, placement)
    placement_ref[...] = placement.astype(bf16)
    hidden = sums_ref[0] + sums_ref[1]
    hidden_ref[...] = hidden
    width = hidden.shape[1]
    gained = hidden * gain_ref[...]
    squares = jnp.sum(hidden * hidden, axis=1, keepdims=True)
    square_high = squares.astype(bf16).astype(f32)
    logits = lax.dot_general(
        gained,
        router_ref[...],
        (((1,), (1,)), ((), ())),
        preferred_element_type=f32,
        precision=lax.Precision.HIGHEST,
    )
    spread_out = jnp.concatenate([logits, jnp.zeros((rows, 128 - expert_total), f32)], axis=1)
    logit_high = spread_out.astype(bf16).astype(f32)
    first = width % 128
    side = pltpu.roll(logit_high, first, 1) + pltpu.roll(
        spread_out - logit_high, first + expert_total, 1
    )
    side = side + pltpu.roll(named, first + 2 * expert_total, 1)
    side = jnp.where(lane == first + 3 * expert_total, square_high, side)
    side = jnp.where(lane == first + 3 * expert_total + 1, squares - square_high, side)
    full = width - first
    last = jnp.concatenate([gained[:, full:], jnp.zeros((rows, 128 - first), f32)], axis=1)
    content = jnp.concatenate([gained[:, :full], jnp.where(lane < first, last, side)], axis=1)
    out = lax.dot_general(
        placement.astype(bf16),
        content.astype(bf16),
        (((0,), (0,)), ((), ())),
        preferred_element_type=f32,
    )
    buffer_ref[...] = out.astype(bf16).reshape(buffer_ref.shape)


def project_kernel(gathered_ref, weight_ref, out_ref):
    members, groups, width = gathered_ref.shape
    total = members * groups
    rows = gathered_ref[...].reshape(total, width)
    target = iota((total, total), 0)
    source = iota((total, total), 1)
    wanted = (target >> 3 & 1) * (total // 2) + (target >> 4) * 8 + (target & 7)
    found = (source & (groups - 1)) * members + (source >> 4)
    rows = select_rows(one_hot(wanted == found), rows)
    out = dot_nt(rows, weight_ref[...]).astype(bf16)
    out_ref[...] = out.reshape(out_ref.shape)


def gate_up_kernel(expert_total, expert_ref, received_ref, weight_ref, out_ref):
    members, chunk, width = received_ref.shape
    total = members * chunk
    rows = received_ref[...].reshape(total, width)
    shape = (24 * members, total)
    target = iota(shape, 0)
    source = iota(shape, 1)
    base = 24 * (source >> 4)
    slot = source & 15
    gate_rows = select_rows(one_hot((target == base + slot) & (slot < 12)), rows)
    place = base + jnp.where(slot < 8, slot + 16, slot + 4)
    up_rows = select_rows(one_hot((target == place) & (slot < 12)), rows)
    left = jnp.concatenate([gate_rows, up_rows], axis=1)
    sums = jnp.dot(left, weight_ref[...], preferred_element_type=f32)
    side = received_ref[:, :, width - 128 :].astype(f32)
    first = iota((8, 128), 1) < 64
    is_expert = (iota((8, 128), 1) & 63) == 3 * expert_total + 2
    expert = expert_ref[0].astype(f32)
    columns = sums.shape[1] // 128
    for member in range(members):
        tiles = [
            sums[24 * member + 8 * row : 24 * member + 8 * row + 8, 128 * col : 128 * col + 128]
            for row in range(3)
            for col in range(columns)
        ]
        turned = pltpu.roll(side[member, :8], 64, 1)
        last = jnp.where(first, turned, side[member, 8:])
        tiles.append(jnp.where(is_expert, expert, last))
        out_ref[member] = jnp.concatenate(tiles, axis=0).astype(bf16)


def activate_kernel(model_width, expert_total, sums_ref, out_ref):
    members, height, _ = sums_ref.shape
    columns = height // 24
    total = sums_ref[0].astype(f32)
    for member in range(1, members):
        total = total + sums_ref[member].astype(f32)

    def block(row):
        first = 8 * columns * row
        return jnp.concatenate(
            [total[first + 8 * col : first + 8 * col + 8] for col in range(columns)], axis=1
        )

    side = total[24 * columns :]
    side = jnp.concatenate([side, pltpu.roll(side, 64, 1)], axis=0)
    lane = iota(side.shape, 1)
    logits = side + pltpu.roll(side, 128 - expert_total, 1)
    named = pltpu.roll(side, 128 - 2 * expert_total, 1)
    square_lane = 3 * expert_total
    is_square = (lane == square_lane) | (lane == square_lane + 1)
    squares = jnp.sum(jnp.where(is_square, side, 0.0), axis=1, keepdims=True)
    inverse_rms = lax.rsqrt(squares / model_width + norm_eps)
    scores = 1.0 / (1.0 + jnp.exp(-jnp.where(lane < expert_total, logits * inverse_rms, 0.0)))
    chosen = (named > 0.5) & (lane < expert_total)
    expert = jnp.sum(jnp.where(lane == square_lane + 2, side, 0.0), axis=1, keepdims=True)
    is_own = lane.astype(f32) * members == expert
    picked = jnp.sum(jnp.where(is_own, scores, 0.0), axis=1, keepdims=True)
    denominator = jnp.sum(jnp.where(chosen, scores, 0.0), axis=1, keepdims=True)
    occupied = denominator > 0.0
    weight = route_scale * picked / jnp.where(occupied, denominator, 1.0)
    weight = jnp.where(occupied, weight, 0.0)

    def activation(gate, up, scale, share):
        gate = gate * scale
        return gate / (1.0 + jnp.exp(-gate)) * (up * scale) * share

    early = activation(block(0), block(2), inverse_rms[:8], weight[:8])
    mixed = block(1)
    late = activation(mixed, pltpu.roll(mixed, 4, 0), inverse_rms[8:], weight[8:])
    half = early.shape[1] // 2
    last = jnp.where(
        iota((8, half), 0) < 4, late[:, :half], pltpu.roll(late[:, half:], 4, 0)
    )
    packed = jnp.concatenate([early[:, :half], early[:, half:], last], axis=0).astype(bf16)
    for member in range(out_ref.shape[0]):
        out_ref[member] = packed


def down_kernel(packed_ref, weight_ref, out_ref):
    members, height, half = packed_ref.shape
    rows = packed_ref[...].reshape(members * height, half)
    shape = (16 * members, members * height)
    target = iota(shape, 0)
    source = iota(shape, 1)
    base = 24 * (target >> 4)
    slot = target & 15
    low_place = base + jnp.where(slot < 8, slot, slot + 8)
    high_place = base + jnp.where(slot < 8, slot + 8, slot + 12)
    low = select_rows(one_hot((source == low_place) & (slot < 12)), rows)
    high = select_rows(one_hot((source == high_place) & (slot < 12)), rows)
    out = dot_nt(jnp.concatenate([low, high], axis=1), weight_ref[...]).astype(bf16)
    out_ref[...] = out.reshape(out_ref.shape)


def body(
    q_latent,
    q_rope,
    cache_latent,
    cache_rope,
    lengths,
    w_uv,
    w_out,
    resid,
    norm_gain,
    router,
    routes,
    slots,
    w_gateup,
    w_down,
):
    sections = lax.axis_size("sec")
    groups = lax.axis_size("grp")
    members = lax.axis_size("dev")
    section = lax.axis_index("sec")
    _, head_total, latent = q_latent.shape
    hist_local = cache_latent.shape[1]
    rope_width = cache_rope.shape[1]
    half_heads = head_total // sections
    head_block, _, value_width = w_uv.shape
    block_rows, width_local = resid.shape
    choices = routes.shape[1]
    expert_total = router.shape[1]
    capacity = max(2, 3 * block_rows // 4)
    pair_rows = sections * block_rows
    in_smem = pl.BlockSpec(memory_space=pltpu.SMEM)
    vmem = pltpu.CompilerParams(vmem_limit_bytes=32 * 2**20)

    place = jnp.stack([section, lengths[0] - section * hist_local]).astype(jnp.int32)
    sent, kept_part = pl.pallas_call(
        attend_kernel,
        out_shape=(
            jax.ShapeDtypeStruct((half_heads, latent + 128), bf16),
            jax.ShapeDtypeStruct((half_heads, latent + 128), f32),
        ),
        in_specs=[in_smem] + [pl.BlockSpec(memory_space=pl.ANY)] * 4 + in_vmem(2),
        out_specs=tuple(in_vmem(2)),
        scratch_shapes=[
            pltpu.VMEM((head_total, latent), bf16),
            pltpu.VMEM(q_rope.shape, bf16),
            pltpu.VMEM(cache_latent.shape[1:], bf16),
            pltpu.VMEM(cache_rope.shape[1:], bf16),
            pltpu.SemaphoreType.DMA((4,)),
        ],
        compiler_params=vmem,
    )(
        place,
        q_latent[0],
        q_rope,
        cache_latent[0],
        cache_rope[0],
        routes,
        slots,
    )

    other = 1 - section
    both = lax.all_gather(sent, "sec", axis=0)
    theirs = lax.dynamic_index_in_dim(both, other, 0, False)
    top_mine = kept_part[:, latent : latent + 1]
    mass_mine = kept_part[:, latent + 1 : latent + 2] + kept_part[:, latent + 2 : latent + 3]
    top_theirs = theirs[:, latent : latent + 1].astype(f32)
    mass_theirs = (
        theirs[:, latent + 1 : latent + 2].astype(f32)
        + theirs[:, latent + 2 : latent + 3].astype(f32)
    )
    top_both = jnp.maximum(top_mine, top_theirs)
    factor_mine = jnp.exp(top_mine - top_both)
    factor_theirs = jnp.exp(top_theirs - top_both)
    mass_both = mass_mine * factor_mine + mass_theirs * factor_theirs
    latent_out = (
        kept_part[:, :latent] * factor_mine + theirs[:, :latent].astype(f32) * factor_theirs
    ) / mass_both
    latent_out = latent_out.astype(bf16)
    tables = both[:, :block_rows, latent:]

    outgoing_heads = latent_out.reshape(groups, head_block, latent)
    arrived = lax.all_to_all(outgoing_heads, "grp", split_axis=0, concat_axis=0, tiled=True)
    values = jnp.einsum("nhc,hcv->nhv", arrived, w_uv, preferred_element_type=f32).astype(bf16)
    width_heads = head_block * value_width
    gathered = spread(values.reshape(groups, width_heads), "dev")
    partial = pl.pallas_call(
        project_kernel,
        out_shape=jax.ShapeDtypeStruct((groups, pair_rows, width_local), bf16),
        in_specs=in_vmem(2),
        out_specs=in_vmem(1)[0],
        compiler_params=vmem,
    )(gathered, w_out.T)
    partial = lax.all_to_all(partial, "grp", split_axis=0, concat_axis=0, tiled=True)
    summed = pl.pallas_call(
        block_sum_kernel,
        out_shape=jax.ShapeDtypeStruct((pair_rows, width_local), f32),
        in_specs=[in_smem] + in_vmem(2),
        out_specs=in_vmem(1)[0],
        compiler_params=vmem,
    )(place, partial, resid)
    summed = lax.all_gather(summed, "sec", axis=0)

    chunk = 16
    padded_width = width_local + -width_local % 128
    buffer, hidden, placement = pl.pallas_call(
        functools.partial(dispatch_kernel, expert_total, choices, capacity),
        out_shape=(
            jax.ShapeDtypeStruct((expert_total, chunk, padded_width), bf16),
            jax.ShapeDtypeStruct((pair_rows, width_local), f32),
            jax.ShapeDtypeStruct((pair_rows, expert_total * chunk), bf16),
        ),
        in_specs=in_vmem(4),
        out_specs=tuple(in_vmem(3)),
        compiler_params=vmem,
    )(summed, norm_gain[None], router.T, tables)
    received = lax.all_to_all(buffer, "grp", split_axis=0, concat_axis=0, tiled=True)

    unit = w_gateup.shape[3]
    weight = jnp.pad(
        w_gateup[0].transpose(1, 0, 2), ((0, 0), (0, padded_width - width_local), (0, 0))
    ).reshape(2 * padded_width, unit)
    sums = pl.pallas_call(
        functools.partial(gate_up_kernel, expert_total),
        out_shape=jax.ShapeDtypeStruct((members, 24 * unit // 128 + 8, 128), bf16),
        in_specs=[in_smem] + in_vmem(2),
        out_specs=in_vmem(1)[0],
        compiler_params=vmem,
    )(lax.axis_index("grp").reshape(1), received, weight)
    sums = lax.all_to_all(sums, "dev", split_axis=0, concat_axis=0, tiled=True)
    packed = pl.pallas_call(
        functools.partial(activate_kernel, width_local * members, expert_total),
        out_shape=jax.ShapeDtypeStruct((members, 24, unit // 2), bf16),
        in_specs=in_vmem(1),
        out_specs=in_vmem(1)[0],
        compiler_params=vmem,
    )(sums)

    everyone = lax.all_to_all(packed, "dev", split_axis=0, concat_axis=0, tiled=True)
    down = pl.pallas_call(
        down_kernel,
        out_shape=jax.ShapeDtypeStruct((groups, chunk, width_local), bf16),
        in_specs=in_vmem(2),
        out_specs=in_vmem(1)[0],
        compiler_params=vmem,
    )(everyone, w_down[0].T)
    returned = lax.all_to_all(down, "grp", split_axis=0, concat_axis=0, tiled=True)
    returned = returned.reshape(expert_total * chunk, width_local)
    mixture = jnp.dot(placement, returned, preferred_element_type=f32)
    halves = lax.all_gather(mixture, "sec", axis=0)
    return pl.pallas_call(
        last_sum_kernel,
        out_shape=jax.ShapeDtypeStruct((block_rows, width_local), bf16),
        in_specs=[in_smem] + in_vmem(2),
        out_specs=in_vmem(1)[0],
        compiler_params=vmem,
    )(place, halves, hidden)


def solution(mesh):
    in_specs = (
        P(("grp", "dev"), None, None),
        P(("grp", "dev"), None),
        P(("grp", "dev"), "sec", None),
        P(("grp", "dev"), None, "sec"),
        P(("grp", "dev")),
        P(("sec", "grp"), None, None),
        P(("sec", "grp"), "dev"),
        P(("sec", "grp"), "dev"),
        P("dev"),
        P("dev", None),
        P(("sec", "grp"), None),
        P(("sec", "grp"), None),
        P("grp", "dev", None, "sec"),
        P("grp", "sec", "dev"),
    )
    out_specs = P(("sec", "grp"), "dev")
    return jax.shard_map(body, mesh=mesh, in_specs=in_specs, out_specs=out_specs, check_vma=False)
```

```python
import functools

import jax
import jax.numpy as jnp
from jax import lax
from jax.experimental import pallas as pl
from jax.experimental.pallas import tpu as pltpu
from jax.sharding import PartitionSpec as P

score_scale = 0.07216878364870323
route_scale = 2.5
norm_eps = 1e-06
masked_floor = -1e30
f32 = jnp.float32
bf16 = jnp.bfloat16


def spread(value, axis):
    copies = jnp.broadcast_to(value[None], (lax.axis_size(axis),) + value.shape)
    return lax.all_to_all(copies, axis, split_axis=0, concat_axis=0, tiled=True)


def in_vmem(count):
    return [pl.BlockSpec(memory_space=pltpu.VMEM) for _ in range(count)]


def iota(shape, axis):
    return lax.broadcasted_iota(jnp.int32, shape, axis)


def one_hot(condition):
    return jnp.where(condition, 1.0, 0.0).astype(bf16)


def select_rows(selection, rows):
    return jnp.dot(selection, rows, preferred_element_type=f32).astype(bf16)


def dot_nt(left, right):
    return lax.dot_general(left, right, (((1,), (1,)), ((), ())), preferred_element_type=f32)


def pad_lanes(value):
    spare = -value.shape[1] % 128
    if spare == 0:
        return value
    return jnp.concatenate([value, jnp.zeros((value.shape[0], spare), value.dtype)], axis=1)


def pack_pair(upper, lower):
    full = upper.shape[1] // 128 * 128
    tiles = [block[:, at : at + 128] for block in (upper, lower) for at in range(0, full, 128)]
    tail = pad_lanes(upper[:, full:]) + pltpu.roll(pad_lanes(lower[:, full:]), 64, 1)
    return jnp.concatenate(tiles + [tail], axis=0)


def unpack_pair(packed):
    full = packed.shape[0] // 16
    tiles = [packed[8 * at : 8 * at + 8] for at in range(2 * full + 1)]
    first = iota((8, 128), 1) < 64
    upper = jnp.concatenate(tiles[:full] + [jnp.where(first, tiles[-1], 0.0)], axis=1)
    turned = pltpu.roll(tiles[-1], 64, 1)
    lower = jnp.concatenate(tiles[full:-1] + [jnp.where(first, turned, 0.0)], axis=1)
    return jnp.concatenate([upper, lower], axis=0)


def pack_slots(upper, lower):
    half = upper.shape[1] // 2
    last = jnp.where(
        iota((8, half), 0) < 4, lower[:, :half], pltpu.roll(lower[:, half:], 4, 0)
    )
    return jnp.concatenate([upper[:, :half], upper[:, half:], last], axis=0)


def unpack_slots(packed):
    last = packed[16:]
    upper = jnp.concatenate([packed[:8], packed[8:16]], axis=1)
    return upper, jnp.concatenate([last, pltpu.roll(last, 4, 0)], axis=1)


def attend_kernel(
    place_ref,
    latent_hbm,
    rope_hbm,
    cache_hbm,
    cache_rope_hbm,
    routes_hbm,
    slots_hbm,
    sent_ref,
    kept_ref,
    routes_ref,
    slots_ref,
    latent_ref,
    rope_ref,
    cache_ref,
    cache_rope_ref,
    sems,
):
    copies = [
        pltpu.make_async_copy(source, target, sems.at[index])
        for index, (source, target) in enumerate(
            [
                (rope_hbm, rope_ref),
                (cache_rope_hbm, cache_rope_ref),
                (latent_hbm, latent_ref),
                (cache_hbm, cache_ref),
                (routes_hbm, routes_ref),
                (slots_hbm, slots_ref),
            ]
        )
    ]
    for copy in copies:
        copy.start()
    copies[4].wait()
    copies[5].wait()
    heads, latent = latent_ref.shape
    half = heads // 2
    width = cache_rope_ref.shape[0]
    mine = pl.multiple_of(place_ref[0] * half, half)
    other = pl.multiple_of(half - place_ref[0] * half, half)

    choices = routes_ref.shape[1]
    spot = iota((choices, 128), 1) - iota((choices, 128), 0)
    table = jnp.dot(
        routes_ref[...].astype(f32), jnp.where(spot == 16, 1.0, 0.0), preferred_element_type=f32
    ) + jnp.dot(
        slots_ref[...].astype(f32), jnp.where(spot == 16 + choices, 1.0, 0.0), preferred_element_type=f32
    )

    copies[0].wait()
    row = rope_ref[...].astype(f32)
    pairs = jnp.concatenate(
        [row[:, 128 * pair : 128 * pair + 128] for pair in range(heads * width // 128)], axis=0
    )
    head = iota((heads, heads // 2), 0) + jnp.where(
        iota((heads, heads // 2), 0) < half, other, mine - half
    )
    picked = select_rows(one_hot(head >> 1 == iota((heads, heads // 2), 1)), pairs.astype(bf16))
    lane_half = iota((heads, 128), 1) >> 6
    picked = jnp.where(lane_half == (iota((heads, 128), 0) & 1), picked, jnp.zeros_like(picked))
    copies[1].wait()
    keys = cache_rope_ref[...]
    rope_scores = jnp.dot(
        picked, jnp.concatenate([keys, keys], axis=0), preferred_element_type=f32
    )
    copies[2].wait()
    query = jnp.concatenate([latent_ref[pl.ds(other, half), :], latent_ref[pl.ds(mine, half), :]], axis=0)
    copies[3].wait()
    cache = cache_ref[...]
    scores = dot_nt(query, cache) + rope_scores
    usable = iota(scores.shape, 1) < place_ref[1]
    masked = jnp.where(usable, scores * score_scale, masked_floor)
    top = jnp.max(masked, axis=1, keepdims=True).astype(bf16).astype(f32)
    expon = jnp.where(usable, jnp.exp(masked - top), 0.0)
    mass = jnp.sum(expon, axis=1, keepdims=True)
    weighted = jnp.dot(expon.astype(bf16), cache, preferred_element_type=f32)
    mass_high = mass.astype(bf16).astype(f32)
    lane = iota((heads, 128), 1)
    side = jnp.where(lane == 0, top, 0.0)
    side = jnp.where(lane == 1, mass_high, side)
    side = jnp.where(lane == 2, mass - mass_high, side)
    kept_ref[:, :latent] = weighted[half:]
    kept_ref[:, latent:] = side[half:]
    block_rows = table.shape[0]
    side = jnp.concatenate([side[:block_rows] + table, side[block_rows:half]], axis=0)
    sent_ref[:, :latent] = weighted[:half].astype(bf16)
    sent_ref[:, latent:] = side.astype(bf16)


def block_sum_kernel(section_ref, partial_ref, resid_ref, out_ref):
    total = partial_ref[0].astype(f32)
    for group in range(1, partial_ref.shape[0]):
        total = total + partial_ref[group].astype(f32)
    resid = resid_ref[...].astype(f32)
    section = section_ref[...]
    upper = jnp.where(section == 0, resid, 0.0)
    lower = jnp.where(section == 1, resid, 0.0)
    out_ref[...] = total + pack_pair(upper, lower)


def last_sum_kernel(section_ref, halves_ref, hidden_ref, out_ref):
    block_rows, width = out_ref.shape
    total = halves_ref[0] + halves_ref[1]
    rows = total.shape[0] // 2
    total = hidden_ref[...] + jnp.concatenate([total[:rows], total[rows:]], axis=1)
    own = jnp.where(section_ref[...] == 0, total[:block_rows], total[block_rows:])
    out_ref[...] = own[:, :width].astype(bf16)


def dispatch_kernel(
    expert_total, choices, capacity, sums_ref, gain_ref, router_ref, both_ref, buffer_ref, hidden_ref, placement_ref
):
    latent = both_ref.shape[2] - 128
    table = both_ref[:, :8, latent:].astype(f32).reshape(16, 128)
    rows = table.shape[0]
    chunk = buffer_ref.shape[1]
    lane = iota((rows, 128), 1)
    block = jnp.where(iota((rows, 1), 0) < rows // 2, 0.0, 1.0 * capacity)
    named = jnp.zeros((rows, 128), f32)
    spot = iota((rows, expert_total * chunk), 1).astype(f32)
    low = jnp.zeros(spot.shape, f32)
    high = jnp.zeros(spot.shape, f32)
    for choice in range(choices):
        route = table[:, 16 + choice : 17 + choice]
        slot = table[:, 16 + choices + choice : 17 + choices + choice]
        named = jnp.where(lane.astype(f32) == route, 1.0, named)
        packed = block + slot
        early = packed < 8
        kept = slot < capacity
        start = route * chunk + packed
        low_spot = jnp.where(kept, start + jnp.where(early, 0.0, 8.0), -1.0)
        high_spot = jnp.where(kept, start + jnp.where(early, 8.0, 12.0), -1.0)
        low = jnp.where(spot == low_spot, 1.0, low)
        high = jnp.where(spot == high_spot, 1.0, high)
    placement = jnp.concatenate([low, high], axis=0).astype(bf16)
    placement_ref[...] = placement

    hidden = unpack_pair(sums_ref[0] + sums_ref[1])
    hidden_ref[...] = hidden
    width = gain_ref.shape[1]
    gained = hidden * pad_lanes(gain_ref[...])
    squares = jnp.sum(hidden * hidden, axis=1, keepdims=True)
    square_high = squares.astype(bf16).astype(f32)
    logits = lax.dot_general(
        gained[:, :width],
        router_ref[...],
        (((1,), (1,)), ((), ())),
        preferred_element_type=f32,
        precision=lax.Precision.HIGHEST,
    )
    spread_out = pad_lanes(logits)
    logit_high = spread_out.astype(bf16).astype(f32)
    first = width % 128
    side = pltpu.roll(logit_high, first, 1) + pltpu.roll(
        spread_out - logit_high, first + expert_total, 1
    )
    side = side + pltpu.roll(named, first + 2 * expert_total, 1)
    side = jnp.where(lane == first + 3 * expert_total, square_high, side)
    side = jnp.where(lane == first + 3 * expert_total + 1, squares - square_high, side)
    full = width - first
    last = jnp.where(lane < first, gained[:, full:], side)
    content = jnp.concatenate([gained[:, :full], last], axis=1)
    half = content.shape[1] // 2
    content = jnp.concatenate([content[:, :half], content[:, half:]], axis=0)
    out = lax.dot_general(
        placement, content.astype(bf16), (((0,), (0,)), ((), ())), preferred_element_type=f32
    )
    buffer_ref[...] = out.astype(bf16).reshape(buffer_ref.shape)


def project_kernel(gathered_ref, weight_ref, out_ref):
    members, groups, width = gathered_ref.shape
    total = members * groups
    rows = gathered_ref[...].reshape(total, width)
    target = iota((total, total), 0)
    source = iota((total, total), 1)
    wanted = (target >> 3 & 1) * (total // 2) + (target >> 4) * 8 + (target & 7)
    found = (source & (groups - 1)) * members + (source >> 4)
    rows = select_rows(one_hot(wanted == found), rows)
    out = dot_nt(rows, weight_ref[...])
    for owner in range(out_ref.shape[0]):
        start = 16 * owner
        packed = pack_pair(out[start : start + 8], out[start + 8 : start + 16])
        out_ref[owner] = packed.astype(bf16)


def gate_up_kernel(expert_total, expert_ref, received_ref, weight_ref, out_ref):
    members = received_ref.shape[0]
    width = 2 * received_ref.shape[2]
    zeros = jnp.zeros((8, width), f32)
    upside = iota((8, width), 0) < 4
    gate_rows, up_rows, side = [], [], []
    first = iota((8, 128), 1) < 64
    is_expert = (iota((8, 128), 1) & 63) == 3 * expert_total + 2
    expert = expert_ref[...].astype(f32)
    for member in range(members):
        early, late = unpack_slots(received_ref[member].astype(f32))
        late = jnp.where(upside, late, 0.0)
        gate_rows += [early, late, zeros]
        up_rows += [zeros, pltpu.roll(late, 4, 0), early]
        turned = pltpu.roll(early[:, width - 128 :], 64, 1)
        last = jnp.where(first, turned, late[:, width - 128 :])
        side.append(jnp.where(is_expert, expert, last))
    left = jnp.concatenate(
        [jnp.concatenate(gate_rows, axis=0), jnp.concatenate(up_rows, axis=0)], axis=1
    ).astype(bf16)
    sums = jnp.dot(left, weight_ref[...], preferred_element_type=f32)
    columns = sums.shape[1] // 128
    for member in range(members):
        tiles = [
            sums[24 * member + 8 * row : 24 * member + 8 * row + 8, 128 * col : 128 * col + 128]
            for row in range(3)
            for col in range(columns)
        ]
        out_ref[member] = jnp.concatenate(tiles + [side[member]], axis=0).astype(bf16)


def activate_kernel(model_width, expert_total, sums_ref, out_ref):
    members, height, _ = sums_ref.shape
    columns = height // 24
    total = sums_ref[0].astype(f32)
    for member in range(1, members):
        total = total + sums_ref[member].astype(f32)

    def block(row):
        first = 8 * columns * row
        return jnp.concatenate(
            [total[first + 8 * col : first + 8 * col + 8] for col in range(columns)], axis=1
        )

    side = total[24 * columns :]
    side = jnp.concatenate([side, pltpu.roll(side, 64, 1)], axis=0)
    lane = iota(side.shape, 1)
    logits = side + pltpu.roll(side, 128 - expert_total, 1)
    named = pltpu.roll(side, 128 - 2 * expert_total, 1)
    square_lane = 3 * expert_total
    is_square = (lane == square_lane) | (lane == square_lane + 1)
    squares = jnp.sum(jnp.where(is_square, side, 0.0), axis=1, keepdims=True)
    inverse_rms = lax.rsqrt(squares / model_width + norm_eps)
    scores = 1.0 / (1.0 + jnp.exp(-jnp.where(lane < expert_total, logits * inverse_rms, 0.0)))
    chosen = (named > 0.5) & (lane < expert_total)
    expert = jnp.sum(jnp.where(lane == square_lane + 2, side, 0.0), axis=1, keepdims=True)
    is_own = lane.astype(f32) * members == expert
    picked = jnp.sum(jnp.where(is_own, scores, 0.0), axis=1, keepdims=True)
    denominator = jnp.sum(jnp.where(chosen, scores, 0.0), axis=1, keepdims=True)
    occupied = denominator > 0.0
    weight = route_scale * picked / jnp.where(occupied, denominator, 1.0)
    weight = jnp.where(occupied, weight, 0.0)

    def activation(gate, up, scale, share):
        gate = gate * scale
        return gate / (1.0 + jnp.exp(-gate)) * (up * scale) * share

    early = activation(block(0), block(2), inverse_rms[:8], weight[:8])
    mixed = block(1)
    late = activation(mixed, pltpu.roll(mixed, 4, 0), inverse_rms[8:], weight[8:])
    packed = pack_slots(early, late).astype(bf16)
    for member in range(out_ref.shape[0]):
        out_ref[member] = packed


def down_kernel(packed_ref, weight_ref, out_ref):
    rows = []
    for member in range(packed_ref.shape[0]):
        rows += unpack_slots(packed_ref[member].astype(f32))
    left = jnp.concatenate(rows, axis=0).astype(bf16)
    out = pad_lanes(dot_nt(left, weight_ref[...]))
    for group in range(out_ref.shape[0]):
        start = 16 * group
        packed = pack_slots(out[start : start + 8], out[start + 8 : start + 16])
        out_ref[group] = packed.astype(bf16)


def body(
    q_latent,
    q_rope,
    cache_latent,
    cache_rope,
    lengths,
    w_uv,
    w_out,
    resid,
    norm_gain,
    router,
    routes,
    slots,
    w_gateup,
    w_down,
):
    sections = lax.axis_size("sec")
    groups = lax.axis_size("grp")
    members = lax.axis_size("dev")
    section = lax.axis_index("sec")
    _, head_total, latent = q_latent.shape
    hist_local = cache_latent.shape[1]
    rope_width = cache_rope.shape[1]
    half_heads = head_total // sections
    head_block, _, value_width = w_uv.shape
    block_rows, width_local = resid.shape
    choices = routes.shape[1]
    expert_total = router.shape[1]
    capacity = max(2, 3 * block_rows // 4)
    pair_rows = sections * block_rows
    pair_tiles = 8 * (2 * (width_local // 128) + 1)
    padded_width = width_local + -width_local % 128
    in_smem = pl.BlockSpec(memory_space=pltpu.SMEM)
    vmem = pltpu.CompilerParams(vmem_limit_bytes=32 * 2**20)

    own_section = section.reshape(1, 1)
    place = jnp.stack([section, lengths[0] - section * hist_local]).astype(jnp.int32)
    sent, kept_part = pl.pallas_call(
        attend_kernel,
        out_shape=(
            jax.ShapeDtypeStruct((half_heads, latent + 128), bf16),
            jax.ShapeDtypeStruct((half_heads, latent + 128), f32),
        ),
        in_specs=[in_smem] + [pl.BlockSpec(memory_space=pltpu.HBM)] * 6,
        out_specs=tuple(in_vmem(2)),
        scratch_shapes=[
            pltpu.VMEM(routes.shape, jnp.int32),
            pltpu.VMEM(slots.shape, jnp.int32),
            pltpu.VMEM((head_total, latent), bf16),
            pltpu.VMEM(q_rope.shape, bf16),
            pltpu.VMEM(cache_latent.shape[1:], bf16),
            pltpu.VMEM(cache_rope.shape[1:], bf16),
            pltpu.SemaphoreType.DMA((6,)),
        ],
        compiler_params=pltpu.CompilerParams(vmem_limit_bytes=60 * 2**20),
    )(
        place,
        q_latent[0],
        q_rope,
        cache_latent[0],
        cache_rope[0],
        routes,
        slots,
    )

    other = 1 - section
    both = lax.all_gather(sent, "sec", axis=0)
    theirs = lax.dynamic_index_in_dim(both, other, 0, False)
    top_mine = kept_part[:, latent : latent + 1]
    mass_mine = kept_part[:, latent + 1 : latent + 2] + kept_part[:, latent + 2 : latent + 3]
    top_theirs = theirs[:, latent : latent + 1].astype(f32)
    mass_theirs = (
        theirs[:, latent + 1 : latent + 2].astype(f32)
        + theirs[:, latent + 2 : latent + 3].astype(f32)
    )
    top_both = jnp.maximum(top_mine, top_theirs)
    factor_mine = jnp.exp(top_mine - top_both)
    factor_theirs = jnp.exp(top_theirs - top_both)
    mass_both = mass_mine * factor_mine + mass_theirs * factor_theirs
    latent_out = (
        kept_part[:, :latent] * factor_mine + theirs[:, :latent].astype(f32) * factor_theirs
    ) / mass_both
    latent_out = latent_out.astype(bf16)

    outgoing_heads = latent_out.reshape(groups, head_block, latent)
    arrived = lax.all_to_all(outgoing_heads, "grp", split_axis=0, concat_axis=0, tiled=True)
    values = jnp.einsum("nhc,hcv->nhv", arrived, w_uv, preferred_element_type=f32).astype(bf16)
    width_heads = head_block * value_width
    gathered = spread(values.reshape(groups, width_heads), "dev")
    partial = pl.pallas_call(
        project_kernel,
        out_shape=jax.ShapeDtypeStruct((groups, pair_tiles, 128), bf16),
        in_specs=in_vmem(2),
        out_specs=in_vmem(1)[0],
        compiler_params=vmem,
    )(gathered, w_out.T)
    partial = lax.all_to_all(partial, "grp", split_axis=0, concat_axis=0, tiled=True)
    summed = pl.pallas_call(
        block_sum_kernel,
        out_shape=jax.ShapeDtypeStruct((pair_tiles, 128), f32),
        in_specs=in_vmem(3),
        out_specs=in_vmem(1)[0],
        compiler_params=vmem,
    )(own_section, partial, resid)
    summed = lax.all_gather(summed, "sec", axis=0)

    chunk = 24
    buffer, hidden, placement = pl.pallas_call(
        functools.partial(dispatch_kernel, expert_total, choices, capacity),
        out_shape=(
            jax.ShapeDtypeStruct((expert_total, chunk, padded_width // 2), bf16),
            jax.ShapeDtypeStruct((pair_rows, padded_width), f32),
            jax.ShapeDtypeStruct((2 * pair_rows, expert_total * chunk), bf16),
        ),
        in_specs=in_vmem(4),
        out_specs=tuple(in_vmem(3)),
        compiler_params=vmem,
    )(summed, norm_gain[None], router.T, both)
    received = lax.all_to_all(buffer, "grp", split_axis=0, concat_axis=0, tiled=True)

    unit = w_gateup.shape[3]
    weight = jnp.pad(
        w_gateup[0].transpose(1, 0, 2), ((0, 0), (0, padded_width - width_local), (0, 0))
    ).reshape(2 * padded_width, unit)
    sums = pl.pallas_call(
        functools.partial(gate_up_kernel, expert_total),
        out_shape=jax.ShapeDtypeStruct((members, 24 * unit // 128 + 8, 128), bf16),
        in_specs=in_vmem(3),
        out_specs=in_vmem(1)[0],
        compiler_params=vmem,
    )(lax.axis_index("grp").reshape(1, 1), received, weight)
    sums = lax.all_to_all(sums, "dev", split_axis=0, concat_axis=0, tiled=True)
    packed = pl.pallas_call(
        functools.partial(activate_kernel, width_local * members, expert_total),
        out_shape=jax.ShapeDtypeStruct((members, 24, unit // 2), bf16),
        in_specs=in_vmem(1),
        out_specs=in_vmem(1)[0],
        compiler_params=vmem,
    )(sums)

    everyone = lax.all_to_all(packed, "dev", split_axis=0, concat_axis=0, tiled=True)
    down = pl.pallas_call(
        down_kernel,
        out_shape=jax.ShapeDtypeStruct((groups, chunk, padded_width // 2), bf16),
        in_specs=in_vmem(2),
        out_specs=in_vmem(1)[0],
        compiler_params=vmem,
    )(everyone, w_down[0].T)
    returned = lax.all_to_all(down, "grp", split_axis=0, concat_axis=0, tiled=True)
    returned = returned.reshape(expert_total * chunk, padded_width // 2)
    mixture = jnp.dot(placement, returned, preferred_element_type=f32)
    halves = lax.all_gather(mixture, "sec", axis=0)
    return pl.pallas_call(
        last_sum_kernel,
        out_shape=jax.ShapeDtypeStruct((block_rows, width_local), bf16),
        in_specs=in_vmem(3),
        out_specs=in_vmem(1)[0],
        compiler_params=vmem,
    )(own_section, halves, hidden)


def solution(mesh):
    in_specs = (
        P(("grp", "dev"), None, None),
        P(("grp", "dev"), None),
        P(("grp", "dev"), "sec", None),
        P(("grp", "dev"), None, "sec"),
        P(("grp", "dev")),
        P(("sec", "grp"), None, None),
        P(("sec", "grp"), "dev"),
        P(("sec", "grp"), "dev"),
        P("dev"),
        P("dev", None),
        P(("sec", "grp"), None),
        P(("sec", "grp"), None),
        P("grp", "dev", None, "sec"),
        P("grp", "sec", "dev"),
    )
    out_specs = P(("sec", "grp"), "dev")
    return jax.shard_map(body, mesh=mesh, in_specs=in_specs, out_specs=out_specs, check_vma=False)
```

```python
import functools

import jax
import jax.numpy as jnp
from jax import lax
from jax.experimental import pallas as pl
from jax.experimental.pallas import tpu as pltpu
from jax.sharding import PartitionSpec as P

score_scale = 0.07216878364870323
route_scale = 2.5
norm_eps = 1e-06
masked_floor = -1e30
f32 = jnp.float32
bf16 = jnp.bfloat16


def spread(value, axis):
    copies = jnp.broadcast_to(value[None], (lax.axis_size(axis),) + value.shape)
    return lax.all_to_all(copies, axis, split_axis=0, concat_axis=0, tiled=True)


def in_vmem(count):
    return [pl.BlockSpec(memory_space=pltpu.VMEM) for _ in range(count)]


def iota(shape, axis):
    return lax.broadcasted_iota(jnp.int32, shape, axis)


def one_hot(condition):
    return jnp.where(condition, 1.0, 0.0).astype(bf16)


def select_rows(selection, rows):
    return jnp.dot(selection, rows, preferred_element_type=f32).astype(bf16)


def dot_nt(left, right):
    return lax.dot_general(left, right, (((1,), (1,)), ((), ())), preferred_element_type=f32)


def pad_lanes(value):
    spare = -value.shape[1] % 128
    if spare == 0:
        return value
    return jnp.concatenate([value, jnp.zeros((value.shape[0], spare), value.dtype)], axis=1)


def pack_pair(upper, lower):
    full = upper.shape[1] // 128 * 128
    tiles = [block[:, at : at + 128] for block in (upper, lower) for at in range(0, full, 128)]
    tail = pad_lanes(upper[:, full:]) + pltpu.roll(pad_lanes(lower[:, full:]), 64, 1)
    return jnp.concatenate(tiles + [tail], axis=0)


def unpack_pair(packed):
    full = packed.shape[0] // 16
    tiles = [packed[8 * at : 8 * at + 8] for at in range(2 * full + 1)]
    first = iota((8, 128), 1) < 64
    upper = jnp.concatenate(tiles[:full] + [jnp.where(first, tiles[-1], 0.0)], axis=1)
    turned = pltpu.roll(tiles[-1], 64, 1)
    lower = jnp.concatenate(tiles[full:-1] + [jnp.where(first, turned, 0.0)], axis=1)
    return jnp.concatenate([upper, lower], axis=0)


def pack_slots(upper, lower):
    half = upper.shape[1] // 2
    last = jnp.where(
        iota((8, half), 0) < 4, lower[:, :half], pltpu.roll(lower[:, half:], 4, 0)
    )
    return jnp.concatenate([upper[:, :half], upper[:, half:], last], axis=0)


def unpack_slots(packed):
    last = packed[16:]
    upper = jnp.concatenate([packed[:8], packed[8:16]], axis=1)
    return upper, jnp.concatenate([last, pltpu.roll(last, 4, 0)], axis=1)


def attend_kernel(
    place_ref,
    latent_hbm,
    rope_hbm,
    cache_hbm,
    cache_rope_hbm,
    routes_hbm,
    slots_hbm,
    sent_ref,
    kept_ref,
    routes_ref,
    slots_ref,
    latent_ref,
    rope_ref,
    cache_ref,
    cache_rope_ref,
    sems,
):
    copies = [
        pltpu.make_async_copy(source, target, sems.at[index])
        for index, (source, target) in enumerate(
            [
                (rope_hbm, rope_ref),
                (cache_rope_hbm, cache_rope_ref),
                (latent_hbm, latent_ref),
                (cache_hbm, cache_ref),
                (routes_hbm, routes_ref),
                (slots_hbm, slots_ref),
            ]
        )
    ]
    for copy in copies:
        copy.start()
    copies[4].wait()
    copies[5].wait()
    heads, latent = latent_ref.shape
    half = heads // 2
    width = cache_rope_ref.shape[0]
    mine = pl.multiple_of(place_ref[0] * half, half)
    other = pl.multiple_of(half - place_ref[0] * half, half)

    choices = routes_ref.shape[1]
    spot = iota((choices, 128), 1) - iota((choices, 128), 0)
    table = jnp.dot(
        routes_ref[...].astype(f32), jnp.where(spot == 16, 1.0, 0.0), preferred_element_type=f32
    ) + jnp.dot(
        slots_ref[...].astype(f32), jnp.where(spot == 16 + choices, 1.0, 0.0), preferred_element_type=f32
    )

    copies[0].wait()
    row = rope_ref[...].astype(f32)
    pairs = jnp.concatenate(
        [row[:, 128 * pair : 128 * pair + 128] for pair in range(heads * width // 128)], axis=0
    )
    head = iota((heads, heads // 2), 0) + jnp.where(
        iota((heads, heads // 2), 0) < half, other, mine - half
    )
    picked = select_rows(one_hot(head >> 1 == iota((heads, heads // 2), 1)), pairs.astype(bf16))
    lane_half = iota((heads, 128), 1) >> 6
    picked = jnp.where(lane_half == (iota((heads, 128), 0) & 1), picked, jnp.zeros_like(picked))
    copies[1].wait()
    keys = cache_rope_ref[...]
    rope_scores = jnp.dot(
        picked, jnp.concatenate([keys, keys], axis=0), preferred_element_type=f32
    )
    copies[2].wait()
    query = jnp.concatenate([latent_ref[pl.ds(other, half), :], latent_ref[pl.ds(mine, half), :]], axis=0)
    copies[3].wait()
    cache = cache_ref[...]
    scores = dot_nt(query, cache) + rope_scores
    usable = iota(scores.shape, 1) < place_ref[1]
    masked = jnp.where(usable, scores * score_scale, masked_floor)
    top = jnp.max(masked, axis=1, keepdims=True).astype(bf16).astype(f32)
    expon = jnp.where(usable, jnp.exp(masked - top), 0.0)
    mass = jnp.sum(expon, axis=1, keepdims=True)
    weighted = jnp.dot(expon.astype(bf16), cache, preferred_element_type=f32)
    mass_high = mass.astype(bf16).astype(f32)
    lane = iota((heads, 128), 1)
    side = jnp.where(lane == 0, top, 0.0)
    side = jnp.where(lane == 1, mass_high, side)
    side = jnp.where(lane == 2, mass - mass_high, side)
    kept_ref[:, :latent] = weighted[half:]
    kept_ref[:, latent:] = side[half:]
    block_rows = table.shape[0]
    side = jnp.concatenate([side[:block_rows] + table, side[block_rows:half]], axis=0)
    sent_ref[:, :latent] = weighted[:half].astype(bf16)
    sent_ref[:, latent:] = side.astype(bf16)


def block_sum_kernel(section_ref, partial_ref, resid_ref, out_ref):
    total = partial_ref[0].astype(f32)
    for group in range(1, partial_ref.shape[0]):
        total = total + partial_ref[group].astype(f32)
    resid = resid_ref[...].astype(f32)
    section = section_ref[...]
    upper = jnp.where(section == 0, resid, 0.0)
    lower = jnp.where(section == 1, resid, 0.0)
    out_ref[...] = total + pack_pair(upper, lower)


def last_sum_kernel(section_ref, halves_ref, hidden_ref, out_ref):
    block_rows, width = out_ref.shape
    total = halves_ref[0] + halves_ref[1]
    rows = total.shape[0] // 2
    total = hidden_ref[...] + jnp.concatenate([total[:rows], total[rows:]], axis=1)
    own = jnp.where(section_ref[...] == 0, total[:block_rows], total[block_rows:])
    out_ref[...] = own[:, :width].astype(bf16)


def dispatch_kernel(
    expert_total, choices, capacity, sums_ref, gain_ref, router_ref, both_ref, buffer_ref, hidden_ref, placement_ref
):
    latent = both_ref.shape[2] - 128
    table = both_ref[:, :8, latent:].astype(f32).reshape(16, 128)
    rows = table.shape[0]
    chunk = buffer_ref.shape[1]
    lane = iota((rows, 128), 1)
    block = jnp.where(iota((rows, 1), 0) < rows // 2, 0.0, 1.0 * capacity)
    named = jnp.zeros((rows, 128), f32)
    spot = iota((rows, expert_total * chunk), 1).astype(f32)
    low = jnp.zeros(spot.shape, f32)
    high = jnp.zeros(spot.shape, f32)
    for choice in range(choices):
        route = table[:, 16 + choice : 17 + choice]
        slot = table[:, 16 + choices + choice : 17 + choices + choice]
        named = jnp.where(lane.astype(f32) == route, 1.0, named)
        packed = block + slot
        early = packed < 8
        kept = slot < capacity
        start = route * chunk + packed
        low_spot = jnp.where(kept, start + jnp.where(early, 0.0, 8.0), -1.0)
        high_spot = jnp.where(kept, start + jnp.where(early, 8.0, 12.0), -1.0)
        low = jnp.where(spot == low_spot, 1.0, low)
        high = jnp.where(spot == high_spot, 1.0, high)
    placement = jnp.concatenate([low, high], axis=0).astype(bf16)
    placement_ref[...] = placement

    hidden = unpack_pair(sums_ref[0] + sums_ref[1])
    hidden_ref[...] = hidden
    width = gain_ref.shape[1]
    gained = hidden * pad_lanes(gain_ref[...])
    squares = jnp.sum(hidden * hidden, axis=1, keepdims=True)
    square_high = squares.astype(bf16).astype(f32)
    logits = lax.dot_general(
        gained[:, :width],
        router_ref[...],
        (((1,), (1,)), ((), ())),
        preferred_element_type=f32,
        precision=lax.Precision.HIGHEST,
    )
    spread_out = pad_lanes(logits)
    logit_high = spread_out.astype(bf16).astype(f32)
    first = width % 128
    side = pltpu.roll(logit_high, first, 1) + pltpu.roll(
        spread_out - logit_high, first + expert_total, 1
    )
    side = side + pltpu.roll(named, first + 2 * expert_total, 1)
    side = jnp.where(lane == first + 3 * expert_total, square_high, side)
    side = jnp.where(lane == first + 3 * expert_total + 1, squares - square_high, side)
    full = width - first
    last = jnp.where(lane < first, gained[:, full:], side)
    content = jnp.concatenate([gained[:, :full], last], axis=1)
    half = content.shape[1] // 2
    content = jnp.concatenate([content[:, :half], content[:, half:]], axis=0)
    out = lax.dot_general(
        placement, content.astype(bf16), (((0,), (0,)), ((), ())), preferred_element_type=f32
    )
    buffer_ref[...] = out.astype(bf16).reshape(buffer_ref.shape)


def project_kernel(gathered_ref, weight_ref, out_ref):
    members, groups, width = gathered_ref.shape
    total = members * groups
    rows = gathered_ref[...].reshape(total, width)
    target = iota((total, total), 0)
    source = iota((total, total), 1)
    wanted = (target >> 3 & 1) * (total // 2) + (target >> 4) * 8 + (target & 7)
    found = (source & (groups - 1)) * members + (source >> 4)
    rows = select_rows(one_hot(wanted == found), rows)
    out = dot_nt(rows, weight_ref[...])
    for owner in range(out_ref.shape[0]):
        start = 16 * owner
        packed = pack_pair(out[start : start + 8], out[start + 8 : start + 16])
        out_ref[owner] = packed.astype(bf16)


def gate_up_kernel(expert_total, expert_ref, received_ref, weight_ref, out_ref):
    members = received_ref.shape[0]
    width = 2 * received_ref.shape[2]
    zeros = jnp.zeros((8, width), f32)
    upside = iota((8, width), 0) < 4
    gate_rows, up_rows, side = [], [], []
    first = iota((8, 128), 1) < 64
    is_expert = (iota((8, 128), 1) & 63) == 3 * expert_total + 2
    expert = expert_ref[...].astype(f32)
    for member in range(members):
        early, late = unpack_slots(received_ref[member].astype(f32))
        late = jnp.where(upside, late, 0.0)
        gate_rows += [early, late, zeros]
        up_rows += [zeros, pltpu.roll(late, 4, 0), early]
        turned = pltpu.roll(early[:, width - 128 :], 64, 1)
        last = jnp.where(first, turned, late[:, width - 128 :])
        side.append(jnp.where(is_expert, expert, last))
    left = jnp.concatenate(
        [jnp.concatenate(gate_rows, axis=0), jnp.concatenate(up_rows, axis=0)], axis=1
    ).astype(bf16)
    sums = jnp.dot(left, weight_ref[...], preferred_element_type=f32)
    columns = sums.shape[1] // 128
    for member in range(members):
        tiles = [
            sums[24 * member + 8 * row : 24 * member + 8 * row + 8, 128 * col : 128 * col + 128]
            for row in range(3)
            for col in range(columns)
        ]
        out_ref[member] = jnp.concatenate(tiles + [side[member]], axis=0).astype(bf16)


def activate_kernel(model_width, expert_total, sums_ref, out_ref):
    members, height, _ = sums_ref.shape
    columns = height // 24
    total = sums_ref[0].astype(f32)
    for member in range(1, members):
        total = total + sums_ref[member].astype(f32)

    def block(row):
        first = 8 * columns * row
        return jnp.concatenate(
            [total[first + 8 * col : first + 8 * col + 8] for col in range(columns)], axis=1
        )

    side = total[24 * columns :]
    side = jnp.concatenate([side, pltpu.roll(side, 64, 1)], axis=0)
    lane = iota(side.shape, 1)
    logits = side + pltpu.roll(side, 128 - expert_total, 1)
    named = pltpu.roll(side, 128 - 2 * expert_total, 1)
    square_lane = 3 * expert_total
    is_square = (lane == square_lane) | (lane == square_lane + 1)
    squares = jnp.sum(jnp.where(is_square, side, 0.0), axis=1, keepdims=True)
    inverse_rms = lax.rsqrt(squares / model_width + norm_eps)
    scores = 1.0 / (1.0 + jnp.exp(-jnp.where(lane < expert_total, logits * inverse_rms, 0.0)))
    chosen = (named > 0.5) & (lane < expert_total)
    expert = jnp.sum(jnp.where(lane == square_lane + 2, side, 0.0), axis=1, keepdims=True)
    is_own = lane.astype(f32) * members == expert
    picked = jnp.sum(jnp.where(is_own, scores, 0.0), axis=1, keepdims=True)
    denominator = jnp.sum(jnp.where(chosen, scores, 0.0), axis=1, keepdims=True)
    occupied = denominator > 0.0
    weight = route_scale * picked / jnp.where(occupied, denominator, 1.0)
    weight = jnp.where(occupied, weight, 0.0)

    def activation(gate, up, scale, share):
        gate = gate * scale
        return gate / (1.0 + jnp.exp(-gate)) * (up * scale) * share

    early = activation(block(0), block(2), inverse_rms[:8], weight[:8])
    mixed = block(1)
    late = activation(mixed, pltpu.roll(mixed, 4, 0), inverse_rms[8:], weight[8:])
    packed = pack_slots(early, late).astype(bf16)
    for member in range(out_ref.shape[0]):
        out_ref[member] = packed


def down_kernel(packed_ref, weight_ref, out_ref):
    rows = []
    for member in range(packed_ref.shape[0]):
        rows += unpack_slots(packed_ref[member].astype(f32))
    left = jnp.concatenate(rows, axis=0).astype(bf16)
    out = pad_lanes(dot_nt(left, weight_ref[...]))
    for group in range(out_ref.shape[0]):
        start = 16 * group
        packed = pack_slots(out[start : start + 8], out[start + 8 : start + 16])
        out_ref[group] = packed.astype(bf16)


def body(
    q_latent,
    q_rope,
    cache_latent,
    cache_rope,
    lengths,
    w_uv,
    w_out,
    resid,
    norm_gain,
    router,
    routes,
    slots,
    w_gateup,
    w_down,
):
    sections = lax.axis_size("sec")
    groups = lax.axis_size("grp")
    members = lax.axis_size("dev")
    section = lax.axis_index("sec")
    _, head_total, latent = q_latent.shape
    hist_local = cache_latent.shape[1]
    rope_width = cache_rope.shape[1]
    half_heads = head_total // sections
    head_block, _, value_width = w_uv.shape
    block_rows, width_local = resid.shape
    choices = routes.shape[1]
    expert_total = router.shape[1]
    capacity = max(2, 3 * block_rows // 4)
    pair_rows = sections * block_rows
    pair_tiles = 8 * (2 * (width_local // 128) + 1)
    padded_width = width_local + -width_local % 128
    in_smem = pl.BlockSpec(memory_space=pltpu.SMEM)
    vmem = pltpu.CompilerParams(vmem_limit_bytes=32 * 2**20)

    own_section = section.reshape(1, 1)
    place = jnp.stack([section, lengths[0] - section * hist_local]).astype(jnp.int32)
    sent, kept_part = pl.pallas_call(
        attend_kernel,
        out_shape=(
            jax.ShapeDtypeStruct((half_heads, latent + 128), bf16),
            jax.ShapeDtypeStruct((half_heads, latent + 128), f32),
        ),
        in_specs=[in_smem] + [pl.BlockSpec(memory_space=pltpu.HBM)] * 6,
        out_specs=tuple(in_vmem(2)),
        scratch_shapes=[
            pltpu.VMEM(routes.shape, jnp.int32),
            pltpu.VMEM(slots.shape, jnp.int32),
            pltpu.VMEM((head_total, latent), bf16),
            pltpu.VMEM(q_rope.shape, bf16),
            pltpu.VMEM(cache_latent.shape[1:], bf16),
            pltpu.VMEM(cache_rope.shape[1:], bf16),
            pltpu.SemaphoreType.DMA((6,)),
        ],
        compiler_params=vmem,
    )(
        place,
        *[
            pltpu.with_memory_space_constraint(operand, pltpu.HBM)
            for operand in (q_latent[0], q_rope, cache_latent[0], cache_rope[0], routes, slots)
        ],
    )

    other = 1 - section
    both = lax.all_gather(sent, "sec", axis=0)
    theirs = lax.dynamic_index_in_dim(both, other, 0, False)
    top_mine = kept_part[:, latent : latent + 1]
    mass_mine = kept_part[:, latent + 1 : latent + 2] + kept_part[:, latent + 2 : latent + 3]
    top_theirs = theirs[:, latent : latent + 1].astype(f32)
    mass_theirs = (
        theirs[:, latent + 1 : latent + 2].astype(f32)
        + theirs[:, latent + 2 : latent + 3].astype(f32)
    )
    top_both = jnp.maximum(top_mine, top_theirs)
    factor_mine = jnp.exp(top_mine - top_both)
    factor_theirs = jnp.exp(top_theirs - top_both)
    mass_both = mass_mine * factor_mine + mass_theirs * factor_theirs
    latent_out = (
        kept_part[:, :latent] * factor_mine + theirs[:, :latent].astype(f32) * factor_theirs
    ) / mass_both
    latent_out = latent_out.astype(bf16)

    outgoing_heads = latent_out.reshape(groups, head_block, latent)
    arrived = lax.all_to_all(outgoing_heads, "grp", split_axis=0, concat_axis=0, tiled=True)
    values = jnp.einsum("nhc,hcv->nhv", arrived, w_uv, preferred_element_type=f32).astype(bf16)
    width_heads = head_block * value_width
    gathered = spread(values.reshape(groups, width_heads), "dev")
    partial = pl.pallas_call(
        project_kernel,
        out_shape=jax.ShapeDtypeStruct((groups, pair_tiles, 128), bf16),
        in_specs=in_vmem(2),
        out_specs=in_vmem(1)[0],
        compiler_params=vmem,
    )(gathered, w_out.T)
    partial = lax.all_to_all(partial, "grp", split_axis=0, concat_axis=0, tiled=True)
    summed = pl.pallas_call(
        block_sum_kernel,
        out_shape=jax.ShapeDtypeStruct((pair_tiles, 128), f32),
        in_specs=in_vmem(3),
        out_specs=in_vmem(1)[0],
        compiler_params=vmem,
    )(own_section, partial, resid)
    summed = lax.all_gather(summed, "sec", axis=0)

    chunk = 24
    buffer, hidden, placement = pl.pallas_call(
        functools.partial(dispatch_kernel, expert_total, choices, capacity),
        out_shape=(
            jax.ShapeDtypeStruct((expert_total, chunk, padded_width // 2), bf16),
            jax.ShapeDtypeStruct((pair_rows, padded_width), f32),
            jax.ShapeDtypeStruct((2 * pair_rows, expert_total * chunk), bf16),
        ),
        in_specs=in_vmem(4),
        out_specs=tuple(in_vmem(3)),
        compiler_params=vmem,
    )(summed, norm_gain[None], router.T, both)
    received = lax.all_to_all(buffer, "grp", split_axis=0, concat_axis=0, tiled=True)

    unit = w_gateup.shape[3]
    weight = jnp.pad(
        w_gateup[0].transpose(1, 0, 2), ((0, 0), (0, padded_width - width_local), (0, 0))
    ).reshape(2 * padded_width, unit)
    sums = pl.pallas_call(
        functools.partial(gate_up_kernel, expert_total),
        out_shape=jax.ShapeDtypeStruct((members, 24 * unit // 128 + 8, 128), bf16),
        in_specs=in_vmem(3),
        out_specs=in_vmem(1)[0],
        compiler_params=vmem,
    )(lax.axis_index("grp").reshape(1, 1), received, weight)
    sums = lax.all_to_all(sums, "dev", split_axis=0, concat_axis=0, tiled=True)
    packed = pl.pallas_call(
        functools.partial(activate_kernel, width_local * members, expert_total),
        out_shape=jax.ShapeDtypeStruct((members, 24, unit // 2), bf16),
        in_specs=in_vmem(1),
        out_specs=in_vmem(1)[0],
        compiler_params=vmem,
    )(sums)

    everyone = lax.all_to_all(packed, "dev", split_axis=0, concat_axis=0, tiled=True)
    down = pl.pallas_call(
        down_kernel,
        out_shape=jax.ShapeDtypeStruct((groups, chunk, padded_width // 2), bf16),
        in_specs=in_vmem(2),
        out_specs=in_vmem(1)[0],
        compiler_params=vmem,
    )(everyone, w_down[0].T)
    returned = lax.all_to_all(down, "grp", split_axis=0, concat_axis=0, tiled=True)
    returned = returned.reshape(expert_total * chunk, padded_width // 2)
    mixture = jnp.dot(placement, returned, preferred_element_type=f32)
    halves = lax.all_gather(mixture, "sec", axis=0)
    return pl.pallas_call(
        last_sum_kernel,
        out_shape=jax.ShapeDtypeStruct((block_rows, width_local), bf16),
        in_specs=in_vmem(3),
        out_specs=in_vmem(1)[0],
        compiler_params=vmem,
    )(own_section, halves, hidden)


def solution(mesh):
    in_specs = (
        P(("grp", "dev"), None, None),
        P(("grp", "dev"), None),
        P(("grp", "dev"), "sec", None),
        P(("grp", "dev"), None, "sec"),
        P(("grp", "dev")),
        P(("sec", "grp"), None, None),
        P(("sec", "grp"), "dev"),
        P(("sec", "grp"), "dev"),
        P("dev"),
        P("dev", None),
        P(("sec", "grp"), None),
        P(("sec", "grp"), None),
        P("grp", "dev", None, "sec"),
        P("grp", "sec", "dev"),
    )
    out_specs = P(("sec", "grp"), "dev")
    return jax.shard_map(body, mesh=mesh, in_specs=in_specs, out_specs=out_specs, check_vma=False)
```

```python
import functools

import jax
import jax.numpy as jnp
from jax import lax
from jax.experimental import pallas as pl
from jax.experimental.pallas import tpu as pltpu
from jax.sharding import PartitionSpec as P

score_scale = 0.07216878364870323
route_scale = 2.5
norm_eps = 1e-06
masked_floor = -1e30
f32 = jnp.float32
bf16 = jnp.bfloat16


def spread(value, axis):
    copies = jnp.broadcast_to(value[None], (lax.axis_size(axis),) + value.shape)
    return lax.all_to_all(copies, axis, split_axis=0, concat_axis=0, tiled=True)


def in_vmem(count):
    return [pl.BlockSpec(memory_space=pltpu.VMEM) for _ in range(count)]


def iota(shape, axis):
    return lax.broadcasted_iota(jnp.int32, shape, axis)


def one_hot(condition):
    return jnp.where(condition, 1.0, 0.0).astype(bf16)


def select_rows(selection, rows):
    return jnp.dot(selection, rows, preferred_element_type=f32).astype(bf16)


def dot_nt(left, right):
    return lax.dot_general(left, right, (((1,), (1,)), ((), ())), preferred_element_type=f32)


def pad_lanes(value):
    spare = -value.shape[1] % 128
    if spare == 0:
        return value
    return jnp.concatenate([value, jnp.zeros((value.shape[0], spare), value.dtype)], axis=1)


def pack_pair(upper, lower):
    full = upper.shape[1] // 128 * 128
    tiles = [block[:, at : at + 128] for block in (upper, lower) for at in range(0, full, 128)]
    tail = pad_lanes(upper[:, full:]) + pltpu.roll(pad_lanes(lower[:, full:]), 64, 1)
    return jnp.concatenate(tiles + [tail], axis=0)


def unpack_pair(packed):
    full = packed.shape[0] // 16
    tiles = [packed[8 * at : 8 * at + 8] for at in range(2 * full + 1)]
    first = iota((8, 128), 1) < 64
    upper = jnp.concatenate(tiles[:full] + [jnp.where(first, tiles[-1], 0.0)], axis=1)
    turned = pltpu.roll(tiles[-1], 64, 1)
    lower = jnp.concatenate(tiles[full:-1] + [jnp.where(first, turned, 0.0)], axis=1)
    return jnp.concatenate([upper, lower], axis=0)


def pack_slots(upper, lower):
    half = upper.shape[1] // 2
    last = jnp.where(
        iota((8, half), 0) < 4, lower[:, :half], pltpu.roll(lower[:, half:], 4, 0)
    )
    return jnp.concatenate([upper[:, :half], upper[:, half:], last], axis=0)


def unpack_slots(packed):
    last = packed[16:]
    upper = jnp.concatenate([packed[:8], packed[8:16]], axis=1)
    return upper, jnp.concatenate([last, pltpu.roll(last, 4, 0)], axis=1)


def attend_kernel(
    place_ref,
    latent_hbm,
    rope_hbm,
    cache_hbm,
    cache_rope_hbm,
    routes_hbm,
    slots_hbm,
    sent_ref,
    kept_ref,
    routes_ref,
    slots_ref,
    latent_ref,
    rope_ref,
    cache_ref,
    cache_rope_ref,
    sems,
):
    positions = cache_ref.shape[0]
    step = positions // 4
    blocks = [pl.ds(step * index, step) for index in range(4)]
    copies = [
        pltpu.make_async_copy(source, target, sems.at[index])
        for index, (source, target) in enumerate(
            [
                (rope_hbm, rope_ref),
                (cache_rope_hbm, cache_rope_ref),
                (latent_hbm, latent_ref),
                (routes_hbm, routes_ref),
                (slots_hbm, slots_ref),
            ]
            + [(cache_hbm.at[block], cache_ref.at[block]) for block in blocks]
        )
    ]
    for copy in copies:
        copy.start()
    copies[3].wait()
    copies[4].wait()
    heads, latent = latent_ref.shape
    half = heads // 2
    width = cache_rope_ref.shape[0]
    mine = pl.multiple_of(place_ref[0] * half, half)
    other = pl.multiple_of(half - place_ref[0] * half, half)

    choices = routes_ref.shape[1]
    spot = iota((choices, 128), 1) - iota((choices, 128), 0)
    table = jnp.dot(
        routes_ref[...].astype(f32), jnp.where(spot == 16, 1.0, 0.0), preferred_element_type=f32
    ) + jnp.dot(
        slots_ref[...].astype(f32), jnp.where(spot == 16 + choices, 1.0, 0.0), preferred_element_type=f32
    )

    copies[0].wait()
    row = rope_ref[...].astype(f32)
    pairs = jnp.concatenate(
        [row[:, 128 * pair : 128 * pair + 128] for pair in range(heads * width // 128)], axis=0
    )
    head = iota((heads, heads // 2), 0) + jnp.where(
        iota((heads, heads // 2), 0) < half, other, mine - half
    )
    picked = select_rows(one_hot(head >> 1 == iota((heads, heads // 2), 1)), pairs.astype(bf16))
    lane_half = iota((heads, 128), 1) >> 6
    picked = jnp.where(lane_half == (iota((heads, 128), 0) & 1), picked, jnp.zeros_like(picked))
    copies[1].wait()
    keys = cache_rope_ref[...]
    rope_scores = jnp.dot(
        picked, jnp.concatenate([keys, keys], axis=0), preferred_element_type=f32
    )
    copies[2].wait()
    query = jnp.concatenate([latent_ref[pl.ds(other, half), :], latent_ref[pl.ds(mine, half), :]], axis=0)
    parts = []
    for index, block in enumerate(blocks):
        copies[5 + index].wait()
        parts.append(dot_nt(query, cache_ref[block, :]))
    scores = jnp.concatenate(parts, axis=1) + rope_scores
    usable = iota(scores.shape, 1) < place_ref[1]
    masked = jnp.where(usable, scores * score_scale, masked_floor)
    top = jnp.max(masked, axis=1, keepdims=True).astype(bf16).astype(f32)
    expon = jnp.where(usable, jnp.exp(masked - top), 0.0)
    mass = jnp.sum(expon, axis=1, keepdims=True)
    weighted = jnp.dot(expon.astype(bf16), cache_ref[...], preferred_element_type=f32)
    mass_high = mass.astype(bf16).astype(f32)
    lane = iota((heads, 128), 1)
    side = jnp.where(lane == 0, top, 0.0)
    side = jnp.where(lane == 1, mass_high, side)
    side = jnp.where(lane == 2, mass - mass_high, side)
    kept_ref[:, :latent] = weighted[half:]
    kept_ref[:, latent:] = side[half:]
    block_rows = table.shape[0]
    side = jnp.concatenate([side[:block_rows] + table, side[block_rows:half]], axis=0)
    sent_ref[:, :latent] = weighted[:half].astype(bf16)
    sent_ref[:, latent:] = side.astype(bf16)


def block_sum_kernel(section_ref, partial_ref, resid_ref, out_ref):
    total = partial_ref[0].astype(f32)
    for group in range(1, partial_ref.shape[0]):
        total = total + partial_ref[group].astype(f32)
    resid = resid_ref[...].astype(f32)
    section = section_ref[...]
    upper = jnp.where(section == 0, resid, 0.0)
    lower = jnp.where(section == 1, resid, 0.0)
    out_ref[...] = total + pack_pair(upper, lower)


def last_sum_kernel(section_ref, halves_ref, hidden_ref, out_ref):
    block_rows, width = out_ref.shape
    total = halves_ref[0] + halves_ref[1]
    rows = total.shape[0] // 2
    total = hidden_ref[...] + jnp.concatenate([total[:rows], total[rows:]], axis=1)
    own = jnp.where(section_ref[...] == 0, total[:block_rows], total[block_rows:])
    out_ref[...] = own[:, :width].astype(bf16)


def dispatch_kernel(
    expert_total, choices, capacity, sums_ref, gain_ref, router_ref, both_ref, buffer_ref, hidden_ref, placement_ref
):
    latent = both_ref.shape[2] - 128
    table = both_ref[:, :8, latent:].astype(f32).reshape(16, 128)
    rows = table.shape[0]
    chunk = buffer_ref.shape[1]
    lane = iota((rows, 128), 1)
    block = jnp.where(iota((rows, 1), 0) < rows // 2, 0.0, 1.0 * capacity)
    named = jnp.zeros((rows, 128), f32)
    spot = iota((rows, expert_total * chunk), 1).astype(f32)
    low = jnp.zeros(spot.shape, f32)
    high = jnp.zeros(spot.shape, f32)
    for choice in range(choices):
        route = table[:, 16 + choice : 17 + choice]
        slot = table[:, 16 + choices + choice : 17 + choices + choice]
        named = jnp.where(lane.astype(f32) == route, 1.0, named)
        packed = block + slot
        early = packed < 8
        kept = slot < capacity
        start = route * chunk + packed
        low_spot = jnp.where(kept, start + jnp.where(early, 0.0, 8.0), -1.0)
        high_spot = jnp.where(kept, start + jnp.where(early, 8.0, 12.0), -1.0)
        low = jnp.where(spot == low_spot, 1.0, low)
        high = jnp.where(spot == high_spot, 1.0, high)
    placement = jnp.concatenate([low, high], axis=0).astype(bf16)
    placement_ref[...] = placement

    hidden = unpack_pair(sums_ref[0] + sums_ref[1])
    hidden_ref[...] = hidden
    width = gain_ref.shape[1]
    gained = hidden * pad_lanes(gain_ref[...])
    squares = jnp.sum(hidden * hidden, axis=1, keepdims=True)
    square_high = squares.astype(bf16).astype(f32)
    logits = lax.dot_general(
        gained[:, :width],
        router_ref[...],
        (((1,), (1,)), ((), ())),
        preferred_element_type=f32,
        precision=lax.Precision.HIGHEST,
    )
    spread_out = pad_lanes(logits)
    logit_high = spread_out.astype(bf16).astype(f32)
    first = width % 128
    side = pltpu.roll(logit_high, first, 1) + pltpu.roll(
        spread_out - logit_high, first + expert_total, 1
    )
    side = side + pltpu.roll(named, first + 2 * expert_total, 1)
    side = jnp.where(lane == first + 3 * expert_total, square_high, side)
    side = jnp.where(lane == first + 3 * expert_total + 1, squares - square_high, side)
    full = width - first
    last = jnp.where(lane < first, gained[:, full:], side)
    content = jnp.concatenate([gained[:, :full], last], axis=1)
    half = content.shape[1] // 2
    content = jnp.concatenate([content[:, :half], content[:, half:]], axis=0)
    out = lax.dot_general(
        placement, content.astype(bf16), (((0,), (0,)), ((), ())), preferred_element_type=f32
    )
    buffer_ref[...] = out.astype(bf16).reshape(buffer_ref.shape)


def project_kernel(gathered_ref, weight_ref, out_ref):
    members, groups, width = gathered_ref.shape
    total = members * groups
    rows = gathered_ref[...].reshape(total, width)
    target = iota((total, total), 0)
    source = iota((total, total), 1)
    wanted = (target >> 3 & 1) * (total // 2) + (target >> 4) * 8 + (target & 7)
    found = (source & (groups - 1)) * members + (source >> 4)
    rows = select_rows(one_hot(wanted == found), rows)
    out = dot_nt(rows, weight_ref[...])
    for owner in range(out_ref.shape[0]):
        start = 16 * owner
        packed = pack_pair(out[start : start + 8], out[start + 8 : start + 16])
        out_ref[owner] = packed.astype(bf16)


def gate_up_kernel(expert_total, expert_ref, received_ref, weight_ref, out_ref):
    members = received_ref.shape[0]
    width = 2 * received_ref.shape[2]
    upside = iota((8, width), 0) < 4
    rows, side = [], []
    first = iota((8, 128), 1) < 64
    is_expert = (iota((8, 128), 1) & 63) == 3 * expert_total + 2
    expert = expert_ref[...].astype(f32)
    for member in range(members):
        early, late = unpack_slots(received_ref[member].astype(f32))
        late = jnp.where(upside, late, 0.0)
        rows += [early, late]
        turned = pltpu.roll(early[:, width - 128 :], 64, 1)
        last = jnp.where(first, turned, late[:, width - 128 :])
        side.append(jnp.where(is_expert, expert, last))
    left = jnp.concatenate(rows, axis=0).astype(bf16)
    gate = jnp.dot(left, weight_ref[:width, :], preferred_element_type=f32)
    up = jnp.dot(left, weight_ref[width:, :], preferred_element_type=f32)
    unit = gate.shape[1]
    over = iota((8, unit), 0) < 4
    for member in range(members):
        start = 16 * member
        late_up = pltpu.roll(up[start + 8 : start + 16], 4, 0)
        blocks = [
            gate[start : start + 8],
            jnp.where(over, gate[start + 8 : start + 16], late_up),
            up[start : start + 8],
        ]
        tiles = [block[:, at : at + 128] for block in blocks for at in range(0, unit, 128)]
        out_ref[member] = jnp.concatenate(tiles + [side[member]], axis=0).astype(bf16)


def activate_kernel(model_width, expert_total, sums_ref, out_ref):
    members, height, _ = sums_ref.shape
    columns = height // 24
    total = sums_ref[0].astype(f32)
    for member in range(1, members):
        total = total + sums_ref[member].astype(f32)

    def block(row):
        first = 8 * columns * row
        return jnp.concatenate(
            [total[first + 8 * col : first + 8 * col + 8] for col in range(columns)], axis=1
        )

    side = total[24 * columns :]
    side = jnp.concatenate([side, pltpu.roll(side, 64, 1)], axis=0)
    lane = iota(side.shape, 1)
    logits = side + pltpu.roll(side, 128 - expert_total, 1)
    named = pltpu.roll(side, 128 - 2 * expert_total, 1)
    square_lane = 3 * expert_total
    is_square = (lane == square_lane) | (lane == square_lane + 1)
    squares = jnp.sum(jnp.where(is_square, side, 0.0), axis=1, keepdims=True)
    inverse_rms = lax.rsqrt(squares / model_width + norm_eps)
    scores = 1.0 / (1.0 + jnp.exp(-jnp.where(lane < expert_total, logits * inverse_rms, 0.0)))
    chosen = (named > 0.5) & (lane < expert_total)
    expert = jnp.sum(jnp.where(lane == square_lane + 2, side, 0.0), axis=1, keepdims=True)
    is_own = lane.astype(f32) * members == expert
    picked = jnp.sum(jnp.where(is_own, scores, 0.0), axis=1, keepdims=True)
    denominator = jnp.sum(jnp.where(chosen, scores, 0.0), axis=1, keepdims=True)
    occupied = denominator > 0.0
    weight = route_scale * picked / jnp.where(occupied, denominator, 1.0)
    weight = jnp.where(occupied, weight, 0.0)

    def activation(gate, up, scale, share):
        gate = gate * scale
        return gate / (1.0 + jnp.exp(-gate)) * (up * scale) * share

    early = activation(block(0), block(2), inverse_rms[:8], weight[:8])
    mixed = block(1)
    late = activation(mixed, pltpu.roll(mixed, 4, 0), inverse_rms[8:], weight[8:])
    packed = pack_slots(early, late).astype(bf16)
    for member in range(out_ref.shape[0]):
        out_ref[member] = packed


def down_kernel(packed_ref, weight_ref, out_ref):
    rows = []
    for member in range(packed_ref.shape[0]):
        rows += unpack_slots(packed_ref[member].astype(f32))
    left = jnp.concatenate(rows, axis=0).astype(bf16)
    out = pad_lanes(dot_nt(left, weight_ref[...]))
    for group in range(out_ref.shape[0]):
        start = 16 * group
        packed = pack_slots(out[start : start + 8], out[start + 8 : start + 16])
        out_ref[group] = packed.astype(bf16)


def body(
    q_latent,
    q_rope,
    cache_latent,
    cache_rope,
    lengths,
    w_uv,
    w_out,
    resid,
    norm_gain,
    router,
    routes,
    slots,
    w_gateup,
    w_down,
):
    sections = lax.axis_size("sec")
    groups = lax.axis_size("grp")
    members = lax.axis_size("dev")
    section = lax.axis_index("sec")
    _, head_total, latent = q_latent.shape
    hist_local = cache_latent.shape[1]
    rope_width = cache_rope.shape[1]
    half_heads = head_total // sections
    head_block, _, value_width = w_uv.shape
    block_rows, width_local = resid.shape
    choices = routes.shape[1]
    expert_total = router.shape[1]
    capacity = max(2, 3 * block_rows // 4)
    pair_rows = sections * block_rows
    pair_tiles = 8 * (2 * (width_local // 128) + 1)
    padded_width = width_local + -width_local % 128
    in_smem = pl.BlockSpec(memory_space=pltpu.SMEM)
    vmem = pltpu.CompilerParams(vmem_limit_bytes=32 * 2**20)

    own_section = section.reshape(1, 1)
    place = jnp.stack([section, lengths[0] - section * hist_local]).astype(jnp.int32)
    sent, kept_part = pl.pallas_call(
        attend_kernel,
        out_shape=(
            jax.ShapeDtypeStruct((half_heads, latent + 128), bf16),
            jax.ShapeDtypeStruct((half_heads, latent + 128), f32),
        ),
        in_specs=[in_smem] + [pl.BlockSpec(memory_space=pltpu.HBM)] * 6,
        out_specs=tuple(in_vmem(2)),
        scratch_shapes=[
            pltpu.VMEM(routes.shape, jnp.int32),
            pltpu.VMEM(slots.shape, jnp.int32),
            pltpu.VMEM((head_total, latent), bf16),
            pltpu.VMEM(q_rope.shape, bf16),
            pltpu.VMEM(cache_latent.shape[1:], bf16),
            pltpu.VMEM(cache_rope.shape[1:], bf16),
            pltpu.SemaphoreType.DMA((9,)),
        ],
        compiler_params=vmem,
    )(
        place,
        *[
            pltpu.with_memory_space_constraint(operand, pltpu.HBM)
            for operand in (q_latent[0], q_rope, cache_latent[0], cache_rope[0], routes, slots)
        ],
    )

    other = 1 - section
    both = lax.all_gather(sent, "sec", axis=0)
    theirs = lax.dynamic_index_in_dim(both, other, 0, False)
    top_mine = kept_part[:, latent : latent + 1]
    mass_mine = kept_part[:, latent + 1 : latent + 2] + kept_part[:, latent + 2 : latent + 3]
    top_theirs = theirs[:, latent : latent + 1].astype(f32)
    mass_theirs = (
        theirs[:, latent + 1 : latent + 2].astype(f32)
        + theirs[:, latent + 2 : latent + 3].astype(f32)
    )
    top_both = jnp.maximum(top_mine, top_theirs)
    factor_mine = jnp.exp(top_mine - top_both)
    factor_theirs = jnp.exp(top_theirs - top_both)
    mass_both = mass_mine * factor_mine + mass_theirs * factor_theirs
    latent_out = (
        kept_part[:, :latent] * factor_mine + theirs[:, :latent].astype(f32) * factor_theirs
    ) / mass_both
    latent_out = latent_out.astype(bf16)

    outgoing_heads = latent_out.reshape(groups, head_block, latent)
    arrived = lax.all_to_all(outgoing_heads, "grp", split_axis=0, concat_axis=0, tiled=True)
    values = jnp.einsum("nhc,hcv->nhv", arrived, w_uv, preferred_element_type=f32).astype(bf16)
    width_heads = head_block * value_width
    gathered = spread(values.reshape(groups, width_heads), "dev")
    partial = pl.pallas_call(
        project_kernel,
        out_shape=jax.ShapeDtypeStruct((groups, pair_tiles, 128), bf16),
        in_specs=in_vmem(2),
        out_specs=in_vmem(1)[0],
        compiler_params=vmem,
    )(gathered, w_out.T)
    partial = lax.all_to_all(partial, "grp", split_axis=0, concat_axis=0, tiled=True)
    summed = pl.pallas_call(
        block_sum_kernel,
        out_shape=jax.ShapeDtypeStruct((pair_tiles, 128), f32),
        in_specs=in_vmem(3),
        out_specs=in_vmem(1)[0],
        compiler_params=vmem,
    )(own_section, partial, resid)
    summed = lax.all_gather(summed, "sec", axis=0)

    chunk = 24
    buffer, hidden, placement = pl.pallas_call(
        functools.partial(dispatch_kernel, expert_total, choices, capacity),
        out_shape=(
            jax.ShapeDtypeStruct((expert_total, chunk, padded_width // 2), bf16),
            jax.ShapeDtypeStruct((pair_rows, padded_width), f32),
            jax.ShapeDtypeStruct((2 * pair_rows, expert_total * chunk), bf16),
        ),
        in_specs=in_vmem(4),
        out_specs=tuple(in_vmem(3)),
        compiler_params=vmem,
    )(summed, norm_gain[None], router.T, both)
    received = lax.all_to_all(buffer, "grp", split_axis=0, concat_axis=0, tiled=True)

    unit = w_gateup.shape[3]
    weight = jnp.pad(
        w_gateup[0].transpose(1, 0, 2), ((0, 0), (0, padded_width - width_local), (0, 0))
    ).reshape(2 * padded_width, unit)
    sums = pl.pallas_call(
        functools.partial(gate_up_kernel, expert_total),
        out_shape=jax.ShapeDtypeStruct((members, 24 * unit // 128 + 8, 128), bf16),
        in_specs=in_vmem(3),
        out_specs=in_vmem(1)[0],
        compiler_params=vmem,
    )(lax.axis_index("grp").reshape(1, 1), received, weight)
    sums = lax.all_to_all(sums, "dev", split_axis=0, concat_axis=0, tiled=True)
    packed = pl.pallas_call(
        functools.partial(activate_kernel, width_local * members, expert_total),
        out_shape=jax.ShapeDtypeStruct((members, 24, unit // 2), bf16),
        in_specs=in_vmem(1),
        out_specs=in_vmem(1)[0],
        compiler_params=vmem,
    )(sums)

    everyone = lax.all_to_all(packed, "dev", split_axis=0, concat_axis=0, tiled=True)
    down = pl.pallas_call(
        down_kernel,
        out_shape=jax.ShapeDtypeStruct((groups, chunk, padded_width // 2), bf16),
        in_specs=in_vmem(2),
        out_specs=in_vmem(1)[0],
        compiler_params=vmem,
    )(everyone, w_down[0].T)
    returned = lax.all_to_all(down, "grp", split_axis=0, concat_axis=0, tiled=True)
    returned = returned.reshape(expert_total * chunk, padded_width // 2)
    mixture = jnp.dot(placement, returned, preferred_element_type=f32)
    halves = lax.all_gather(mixture, "sec", axis=0)
    return pl.pallas_call(
        last_sum_kernel,
        out_shape=jax.ShapeDtypeStruct((block_rows, width_local), bf16),
        in_specs=in_vmem(3),
        out_specs=in_vmem(1)[0],
        compiler_params=vmem,
    )(own_section, halves, hidden)


def solution(mesh):
    in_specs = (
        P(("grp", "dev"), None, None),
        P(("grp", "dev"), None),
        P(("grp", "dev"), "sec", None),
        P(("grp", "dev"), None, "sec"),
        P(("grp", "dev")),
        P(("sec", "grp"), None, None),
        P(("sec", "grp"), "dev"),
        P(("sec", "grp"), "dev"),
        P("dev"),
        P("dev", None),
        P(("sec", "grp"), None),
        P(("sec", "grp"), None),
        P("grp", "dev", None, "sec"),
        P("grp", "sec", "dev"),
    )
    out_specs = P(("sec", "grp"), "dev")
    return jax.shard_map(body, mesh=mesh, in_specs=in_specs, out_specs=out_specs, check_vma=False)
```

```python
import functools

import jax
import jax.numpy as jnp
from jax import lax
from jax.experimental import pallas as pl
from jax.experimental.pallas import tpu as pltpu
from jax.sharding import PartitionSpec as P

score_scale = 0.07216878364870323
route_scale = 2.5
norm_eps = 1e-06
masked_floor = -1e30
f32 = jnp.float32
bf16 = jnp.bfloat16


def spread(value, axis):
    copies = jnp.broadcast_to(value[None], (lax.axis_size(axis),) + value.shape)
    return lax.all_to_all(copies, axis, split_axis=0, concat_axis=0, tiled=True)


def in_vmem(count):
    return [pl.BlockSpec(memory_space=pltpu.VMEM) for _ in range(count)]


def iota(shape, axis):
    return lax.broadcasted_iota(jnp.int32, shape, axis)


def one_hot(condition):
    return jnp.where(condition, 1.0, 0.0).astype(bf16)


def select_rows(selection, rows):
    return jnp.dot(selection, rows, preferred_element_type=f32).astype(bf16)


def dot_nt(left, right):
    return lax.dot_general(left, right, (((1,), (1,)), ((), ())), preferred_element_type=f32)


def pad_lanes(value):
    spare = -value.shape[1] % 128
    if spare == 0:
        return value
    return jnp.concatenate([value, jnp.zeros((value.shape[0], spare), value.dtype)], axis=1)


def pack_pair(upper, lower):
    full = upper.shape[1] // 128 * 128
    tiles = [block[:, at : at + 128] for block in (upper, lower) for at in range(0, full, 128)]
    tail = pad_lanes(upper[:, full:]) + pltpu.roll(pad_lanes(lower[:, full:]), 64, 1)
    return jnp.concatenate(tiles + [tail], axis=0)


def unpack_pair(packed):
    full = packed.shape[0] // 16
    tiles = [packed[8 * at : 8 * at + 8] for at in range(2 * full + 1)]
    first = iota((8, 128), 1) < 64
    upper = jnp.concatenate(tiles[:full] + [jnp.where(first, tiles[-1], 0.0)], axis=1)
    turned = pltpu.roll(tiles[-1], 64, 1)
    lower = jnp.concatenate(tiles[full:-1] + [jnp.where(first, turned, 0.0)], axis=1)
    return jnp.concatenate([upper, lower], axis=0)


def pack_slots(upper, lower):
    half = upper.shape[1] // 2
    last = jnp.where(
        iota((8, half), 0) < 4, lower[:, :half], pltpu.roll(lower[:, half:], 4, 0)
    )
    return jnp.concatenate([upper[:, :half], upper[:, half:], last], axis=0)


def unpack_slots(packed):
    last = packed[16:]
    upper = jnp.concatenate([packed[:8], packed[8:16]], axis=1)
    return upper, jnp.concatenate([last, pltpu.roll(last, 4, 0)], axis=1)


def pack_block(value):
    row = iota((8, 128), 0)
    tail = value[:, 384:]
    return jnp.concatenate(
        [
            jnp.where(row < 6, value[:, 128 * at : 128 * at + 128], pltpu.roll(tail, 6 - 2 * at, 0))
            for at in range(3)
        ],
        axis=0,
    )


def attend_kernel(
    place_ref,
    latent_hbm,
    rope_hbm,
    cache_hbm,
    cache_rope_hbm,
    routes_hbm,
    slots_hbm,
    sent_ref,
    kept_ref,
    routes_ref,
    slots_ref,
    latent_ref,
    rope_ref,
    cache_ref,
    cache_rope_ref,
    sems,
):
    copies = [
        pltpu.make_async_copy(source, target, sems.at[index])
        for index, (source, target) in enumerate(
            [
                (rope_hbm, rope_ref),
                (cache_rope_hbm, cache_rope_ref),
                (latent_hbm, latent_ref),
                (cache_hbm, cache_ref),
                (routes_hbm, routes_ref),
                (slots_hbm, slots_ref),
            ]
        )
    ]
    for copy in copies:
        copy.start()
    copies[4].wait()
    copies[5].wait()
    heads, latent = latent_ref.shape
    half = heads // 2
    width = cache_rope_ref.shape[0]
    mine = pl.multiple_of(place_ref[0] * half, half)
    other = pl.multiple_of(half - place_ref[0] * half, half)

    choices = routes_ref.shape[1]
    spot = iota((choices, 128), 1) - iota((choices, 128), 0)
    table = jnp.dot(
        routes_ref[...].astype(f32), jnp.where(spot == 16, 1.0, 0.0), preferred_element_type=f32
    ) + jnp.dot(
        slots_ref[...].astype(f32), jnp.where(spot == 16 + choices, 1.0, 0.0), preferred_element_type=f32
    )

    copies[0].wait()
    row = rope_ref[...].astype(f32)
    pairs = jnp.concatenate(
        [row[:, 128 * pair : 128 * pair + 128] for pair in range(heads * width // 128)], axis=0
    )
    head = iota((heads, heads // 2), 0) + jnp.where(
        iota((heads, heads // 2), 0) < half, other, mine - half
    )
    picked = select_rows(one_hot(head >> 1 == iota((heads, heads // 2), 1)), pairs.astype(bf16))
    lane_half = iota((heads, 128), 1) >> 6
    picked = jnp.where(lane_half == (iota((heads, 128), 0) & 1), picked, jnp.zeros_like(picked))
    copies[1].wait()
    keys = cache_rope_ref[...]
    rope_scores = jnp.dot(
        picked, jnp.concatenate([keys, keys], axis=0), preferred_element_type=f32
    )
    copies[2].wait()
    query = jnp.concatenate([latent_ref[pl.ds(other, half), :], latent_ref[pl.ds(mine, half), :]], axis=0)
    copies[3].wait()
    cache = cache_ref[...]
    scores = dot_nt(query, cache) + rope_scores
    usable = iota(scores.shape, 1) < place_ref[1]
    masked = jnp.where(usable, scores * score_scale, masked_floor)
    top = jnp.max(masked, axis=1, keepdims=True).astype(bf16).astype(f32)
    expon = jnp.where(usable, jnp.exp(masked - top), 0.0)
    mass = jnp.sum(expon, axis=1, keepdims=True)
    weighted = jnp.dot(expon.astype(bf16), cache, preferred_element_type=f32)
    mass_high = mass.astype(bf16).astype(f32)
    lane = iota((heads, 128), 1)
    side = jnp.where(lane == 0, top, 0.0)
    side = jnp.where(lane == 1, mass_high, side)
    side = jnp.where(lane == 2, mass - mass_high, side)
    kept_ref[:, :latent] = weighted[half:]
    kept_ref[:, latent:] = side[half:]
    block_rows = table.shape[0]
    side = jnp.concatenate([side[:block_rows] + table, side[block_rows:half]], axis=0)
    sent_ref[:, :latent] = weighted[:half].astype(bf16)
    sent_ref[:, latent:] = side.astype(bf16)


def block_sum_kernel(section_ref, partial_ref, resid_ref, out_ref):
    total = partial_ref[0].astype(f32)
    for group in range(1, partial_ref.shape[0]):
        total = total + partial_ref[group].astype(f32)
    resid = resid_ref[...].astype(f32)
    section = section_ref[...]
    upper = jnp.where(section == 0, resid, 0.0)
    lower = jnp.where(section == 1, resid, 0.0)
    out_ref[...] = total + pack_pair(upper, lower)


def half_sum_kernel(section_ref, both_ref, kept_ref, out_ref):
    theirs = jnp.where(section_ref[...] == 0, both_ref[1].astype(f32), both_ref[0].astype(f32))
    out_ref[...] = (kept_ref[...] + theirs).astype(bf16)


def last_sum_kernel(returned_ref, placement_ref, hidden_ref, out_ref):
    width = out_ref.shape[1]
    returned = returned_ref[...].reshape(-1, 128)
    tiles = jnp.dot(placement_ref[...], returned, preferred_element_type=f32)
    mixture = jnp.concatenate([tiles[8 * at : 8 * at + 8] for at in range(4)], axis=1)
    out_ref[...] = (hidden_ref[...] + mixture)[:, :width].astype(bf16)


def dispatch_kernel(
    expert_total, choices, capacity, section_ref, sums_ref, gain_ref, router_ref, both_ref, buffer_ref, hidden_ref, placement_ref
):
    latent = both_ref.shape[2] - 128
    table = both_ref[:, :8, latent:].astype(f32).reshape(16, 128)
    rows = table.shape[0]
    chunk = buffer_ref.shape[1]
    lane = iota((rows, 128), 1)
    block = jnp.where(iota((rows, 1), 0) < rows // 2, 0.0, 1.0 * capacity)
    named = jnp.zeros((rows, 128), f32)
    spot = iota((rows, expert_total * chunk), 1).astype(f32)
    low = jnp.zeros(spot.shape, f32)
    high = jnp.zeros(spot.shape, f32)
    for choice in range(choices):
        route = table[:, 16 + choice : 17 + choice]
        slot = table[:, 16 + choices + choice : 17 + choices + choice]
        named = jnp.where(lane.astype(f32) == route, 1.0, named)
        packed = block + slot
        early = packed < 8
        kept = slot < capacity
        start = route * chunk + packed
        low_spot = jnp.where(kept, start + jnp.where(early, 0.0, 8.0), -1.0)
        high_spot = jnp.where(kept, start + jnp.where(early, 8.0, 12.0), -1.0)
        low = jnp.where(spot == low_spot, 1.0, low)
        high = jnp.where(spot == high_spot, 1.0, high)
    placement = jnp.concatenate([low, high], axis=0).astype(bf16)

    is_first = section_ref[...] == 0
    own = jnp.where(is_first, table[:8], table[8:])
    own_spot = iota((8, expert_total * chunk), 1).astype(f32)
    sources = []
    for tile in range(4):
        source = jnp.zeros(own_spot.shape, f32)
        for choice in range(choices):
            route = own[:, 16 + choice : 17 + choice]
            slot = own[:, 16 + choices + choice : 17 + choices + choice]
            if tile < 3:
                wanted = 8.0 * tile + slot
            else:
                pair = jnp.floor(slot * 0.5)
                wanted = 8.0 * pair + 6.0 + (slot - 2.0 * pair)
            wanted = jnp.where(slot < capacity, route * chunk + wanted, -1.0)
            source = jnp.where(own_spot == wanted, 1.0, source)
        sources.append(source)
    placement_ref[...] = jnp.concatenate(sources, axis=0).astype(bf16)

    hidden = unpack_pair(sums_ref[0] + sums_ref[1])
    hidden_ref[...] = jnp.where(is_first, hidden[:8], hidden[8:])
    width = gain_ref.shape[1]
    gained = hidden * pad_lanes(gain_ref[...])
    squares = jnp.sum(hidden * hidden, axis=1, keepdims=True)
    square_high = squares.astype(bf16).astype(f32)
    logits = lax.dot_general(
        gained[:, :width],
        router_ref[...],
        (((1,), (1,)), ((), ())),
        preferred_element_type=f32,
        precision=lax.Precision.HIGHEST,
    )
    spread_out = pad_lanes(logits)
    logit_high = spread_out.astype(bf16).astype(f32)
    first = width % 128
    side = pltpu.roll(logit_high, first, 1) + pltpu.roll(
        spread_out - logit_high, first + expert_total, 1
    )
    side = side + pltpu.roll(named, first + 2 * expert_total, 1)
    side = jnp.where(lane == first + 3 * expert_total, square_high, side)
    side = jnp.where(lane == first + 3 * expert_total + 1, squares - square_high, side)
    full = width - first
    last = jnp.where(lane < first, gained[:, full:], side)
    content = jnp.concatenate([gained[:, :full], last], axis=1)
    half = content.shape[1] // 2
    content = jnp.concatenate([content[:, :half], content[:, half:]], axis=0)
    out = lax.dot_general(
        placement, content.astype(bf16), (((0,), (0,)), ((), ())), preferred_element_type=f32
    )
    buffer_ref[...] = out.astype(bf16).reshape(buffer_ref.shape)


def project_kernel(gathered_ref, weight_ref, out_ref):
    members, groups, width = gathered_ref.shape
    total = members * groups
    rows = gathered_ref[...].reshape(total, width)
    target = iota((total, total), 0)
    source = iota((total, total), 1)
    wanted = (target >> 3 & 1) * (total // 2) + (target >> 4) * 8 + (target & 7)
    found = (source & (groups - 1)) * members + (source >> 4)
    rows = select_rows(one_hot(wanted == found), rows)
    out = dot_nt(rows, weight_ref[...])
    for owner in range(out_ref.shape[0]):
        start = 16 * owner
        packed = pack_pair(out[start : start + 8], out[start + 8 : start + 16])
        out_ref[owner] = packed.astype(bf16)


def gate_up_kernel(expert_total, expert_ref, received_ref, weight_ref, out_ref):
    members = received_ref.shape[0]
    width = 2 * received_ref.shape[2]
    upside = iota((8, width), 0) < 4
    rows, side = [], []
    first = iota((8, 128), 1) < 64
    is_expert = (iota((8, 128), 1) & 63) == 3 * expert_total + 2
    expert = expert_ref[...].astype(f32)
    for member in range(members):
        early, late = unpack_slots(received_ref[member].astype(f32))
        late = jnp.where(upside, late, 0.0)
        rows += [early, late]
        turned = pltpu.roll(early[:, width - 128 :], 64, 1)
        last = jnp.where(first, turned, late[:, width - 128 :])
        side.append(jnp.where(is_expert, expert, last))
    left = jnp.concatenate(rows, axis=0).astype(bf16)
    gate = jnp.dot(left, weight_ref[:width, :], preferred_element_type=f32)
    up = jnp.dot(left, weight_ref[width:, :], preferred_element_type=f32)
    unit = gate.shape[1]
    over = iota((8, unit), 0) < 4
    for member in range(members):
        start = 16 * member
        late_up = pltpu.roll(up[start + 8 : start + 16], 4, 0)
        blocks = [
            gate[start : start + 8],
            jnp.where(over, gate[start + 8 : start + 16], late_up),
            up[start : start + 8],
        ]
        tiles = [block[:, at : at + 128] for block in blocks for at in range(0, unit, 128)]
        out_ref[member] = jnp.concatenate(tiles + [side[member]], axis=0).astype(bf16)


def activate_kernel(model_width, expert_total, sums_ref, out_ref):
    members, height, _ = sums_ref.shape
    columns = height // 24
    total = sums_ref[0].astype(f32)
    for member in range(1, members):
        total = total + sums_ref[member].astype(f32)

    def block(row):
        first = 8 * columns * row
        return jnp.concatenate(
            [total[first + 8 * col : first + 8 * col + 8] for col in range(columns)], axis=1
        )

    side = total[24 * columns :]
    side = jnp.concatenate([side, pltpu.roll(side, 64, 1)], axis=0)
    lane = iota(side.shape, 1)
    logits = side + pltpu.roll(side, 128 - expert_total, 1)
    named = pltpu.roll(side, 128 - 2 * expert_total, 1)
    square_lane = 3 * expert_total
    is_square = (lane == square_lane) | (lane == square_lane + 1)
    squares = jnp.sum(jnp.where(is_square, side, 0.0), axis=1, keepdims=True)
    inverse_rms = lax.rsqrt(squares / model_width + norm_eps)
    scores = 1.0 / (1.0 + jnp.exp(-jnp.where(lane < expert_total, logits * inverse_rms, 0.0)))
    chosen = (named > 0.5) & (lane < expert_total)
    expert = jnp.sum(jnp.where(lane == square_lane + 2, side, 0.0), axis=1, keepdims=True)
    is_own = lane.astype(f32) * members == expert
    picked = jnp.sum(jnp.where(is_own, scores, 0.0), axis=1, keepdims=True)
    denominator = jnp.sum(jnp.where(chosen, scores, 0.0), axis=1, keepdims=True)
    occupied = denominator > 0.0
    weight = route_scale * picked / jnp.where(occupied, denominator, 1.0)
    weight = jnp.where(occupied, weight, 0.0)

    def activation(gate, up, scale, share):
        gate = gate * scale
        return gate / (1.0 + jnp.exp(-gate)) * (up * scale) * share

    early = activation(block(0), block(2), inverse_rms[:8], weight[:8])
    mixed = block(1)
    late = activation(mixed, pltpu.roll(mixed, 4, 0), inverse_rms[8:], weight[8:])
    packed = pack_slots(early, late).astype(bf16)
    for member in range(out_ref.shape[0]):
        out_ref[member] = packed


def down_kernel(section_ref, packed_ref, weight_ref, sent_ref, kept_ref):
    rows = []
    for member in range(packed_ref.shape[0]):
        rows += unpack_slots(packed_ref[member].astype(f32))
    left = jnp.concatenate(rows, axis=0).astype(bf16)
    out = pad_lanes(dot_nt(left, weight_ref[...]))
    is_first = section_ref[...] == 0
    for group in range(sent_ref.shape[0]):
        start = 16 * group
        early, late = out[start : start + 8], out[start + 8 : start + 16]
        row = iota(early.shape, 0)
        second = jnp.where(row < 2, pltpu.roll(early, 2, 0), pltpu.roll(late, 2, 0))
        first, second = pack_block(early), pack_block(second)
        sent_ref[group] = jnp.where(is_first, second, first).astype(bf16)
        kept_ref[group] = jnp.where(is_first, first, second)


def body(
    q_latent,
    q_rope,
    cache_latent,
    cache_rope,
    lengths,
    w_uv,
    w_out,
    resid,
    norm_gain,
    router,
    routes,
    slots,
    w_gateup,
    w_down,
):
    sections = lax.axis_size("sec")
    groups = lax.axis_size("grp")
    members = lax.axis_size("dev")
    section = lax.axis_index("sec")
    _, head_total, latent = q_latent.shape
    hist_local = cache_latent.shape[1]
    rope_width = cache_rope.shape[1]
    half_heads = head_total // sections
    head_block, _, value_width = w_uv.shape
    block_rows, width_local = resid.shape
    choices = routes.shape[1]
    expert_total = router.shape[1]
    capacity = max(2, 3 * block_rows // 4)
    pair_rows = sections * block_rows
    pair_tiles = 8 * (2 * (width_local // 128) + 1)
    padded_width = width_local + -width_local % 128
    in_smem = pl.BlockSpec(memory_space=pltpu.SMEM)
    vmem = pltpu.CompilerParams(vmem_limit_bytes=32 * 2**20)

    own_section = section.reshape(1, 1)
    place = jnp.stack([section, lengths[0] - section * hist_local]).astype(jnp.int32)
    sent, kept_part = pl.pallas_call(
        attend_kernel,
        out_shape=(
            jax.ShapeDtypeStruct((half_heads, latent + 128), bf16),
            jax.ShapeDtypeStruct((half_heads, latent + 128), f32),
        ),
        in_specs=[in_smem] + [pl.BlockSpec(memory_space=pltpu.HBM)] * 6,
        out_specs=tuple(in_vmem(2)),
        scratch_shapes=[
            pltpu.VMEM(routes.shape, jnp.int32),
            pltpu.VMEM(slots.shape, jnp.int32),
            pltpu.VMEM((head_total, latent), bf16),
            pltpu.VMEM(q_rope.shape, bf16),
            pltpu.VMEM(cache_latent.shape[1:], bf16),
            pltpu.VMEM(cache_rope.shape[1:], bf16),
            pltpu.SemaphoreType.DMA((6,)),
        ],
        compiler_params=vmem,
    )(
        place,
        *[
            pltpu.with_memory_space_constraint(operand, pltpu.HBM)
            for operand in (q_latent[0], q_rope, cache_latent[0], cache_rope[0], routes, slots)
        ],
    )

    other = 1 - section
    both = lax.all_gather(sent, "sec", axis=0)
    theirs = lax.dynamic_index_in_dim(both, other, 0, False)
    top_mine = kept_part[:, latent : latent + 1]
    mass_mine = kept_part[:, latent + 1 : latent + 2] + kept_part[:, latent + 2 : latent + 3]
    top_theirs = theirs[:, latent : latent + 1].astype(f32)
    mass_theirs = (
        theirs[:, latent + 1 : latent + 2].astype(f32)
        + theirs[:, latent + 2 : latent + 3].astype(f32)
    )
    top_both = jnp.maximum(top_mine, top_theirs)
    factor_mine = jnp.exp(top_mine - top_both)
    factor_theirs = jnp.exp(top_theirs - top_both)
    mass_both = mass_mine * factor_mine + mass_theirs * factor_theirs
    latent_out = (
        kept_part[:, :latent] * factor_mine + theirs[:, :latent].astype(f32) * factor_theirs
    ) / mass_both
    latent_out = latent_out.astype(bf16)

    outgoing_heads = latent_out.reshape(groups, head_block, latent)
    arrived = lax.all_to_all(outgoing_heads, "grp", split_axis=0, concat_axis=0, tiled=True)
    values = jnp.einsum("nhc,hcv->nhv", arrived, w_uv, preferred_element_type=f32).astype(bf16)
    width_heads = head_block * value_width
    gathered = spread(values.reshape(groups, width_heads), "dev")
    partial = pl.pallas_call(
        project_kernel,
        out_shape=jax.ShapeDtypeStruct((groups, pair_tiles, 128), bf16),
        in_specs=in_vmem(2),
        out_specs=in_vmem(1)[0],
        compiler_params=vmem,
    )(gathered, w_out.T)
    partial = lax.all_to_all(partial, "grp", split_axis=0, concat_axis=0, tiled=True)
    summed = pl.pallas_call(
        block_sum_kernel,
        out_shape=jax.ShapeDtypeStruct((pair_tiles, 128), f32),
        in_specs=in_vmem(3),
        out_specs=in_vmem(1)[0],
        compiler_params=vmem,
    )(own_section, partial, resid)
    summed = lax.all_gather(summed, "sec", axis=0)

    chunk = 24
    buffer, hidden, placement = pl.pallas_call(
        functools.partial(dispatch_kernel, expert_total, choices, capacity),
        out_shape=(
            jax.ShapeDtypeStruct((expert_total, chunk, padded_width // 2), bf16),
            jax.ShapeDtypeStruct((block_rows, padded_width), f32),
            jax.ShapeDtypeStruct((4 * block_rows, expert_total * chunk), bf16),
        ),
        in_specs=in_vmem(5),
        out_specs=tuple(in_vmem(3)),
        compiler_params=vmem,
    )(own_section, summed, norm_gain[None], router.T, both)
    received = lax.all_to_all(buffer, "grp", split_axis=0, concat_axis=0, tiled=True)

    unit = w_gateup.shape[3]
    weight = jnp.pad(
        w_gateup[0].transpose(1, 0, 2), ((0, 0), (0, padded_width - width_local), (0, 0))
    ).reshape(2 * padded_width, unit)
    sums = pl.pallas_call(
        functools.partial(gate_up_kernel, expert_total),
        out_shape=jax.ShapeDtypeStruct((members, 24 * unit // 128 + 8, 128), bf16),
        in_specs=in_vmem(3),
        out_specs=in_vmem(1)[0],
        compiler_params=vmem,
    )(lax.axis_index("grp").reshape(1, 1), received, weight)
    sums = lax.all_to_all(sums, "dev", split_axis=0, concat_axis=0, tiled=True)
    packed = pl.pallas_call(
        functools.partial(activate_kernel, width_local * members, expert_total),
        out_shape=jax.ShapeDtypeStruct((members, 24, unit // 2), bf16),
        in_specs=in_vmem(1),
        out_specs=in_vmem(1)[0],
        compiler_params=vmem,
    )(sums)

    everyone = lax.all_to_all(packed, "dev", split_axis=0, concat_axis=0, tiled=True)
    sent, kept = pl.pallas_call(
        down_kernel,
        out_shape=(
            jax.ShapeDtypeStruct((groups, 24, 128), bf16),
            jax.ShapeDtypeStruct((groups, 24, 128), f32),
        ),
        in_specs=in_vmem(3),
        out_specs=tuple(in_vmem(2)),
        compiler_params=vmem,
    )(own_section, everyone, w_down[0].T)
    halves = lax.all_gather(sent, "sec", axis=0)
    down = pl.pallas_call(
        half_sum_kernel,
        out_shape=jax.ShapeDtypeStruct((groups, 24, 128), bf16),
        in_specs=in_vmem(3),
        out_specs=in_vmem(1)[0],
        compiler_params=vmem,
    )(own_section, halves, kept)
    returned = lax.all_to_all(down, "grp", split_axis=0, concat_axis=0, tiled=True)
    return pl.pallas_call(
        last_sum_kernel,
        out_shape=jax.ShapeDtypeStruct((block_rows, width_local), bf16),
        in_specs=in_vmem(3),
        out_specs=in_vmem(1)[0],
        compiler_params=vmem,
    )(returned, placement, hidden)


def solution(mesh):
    in_specs = (
        P(("grp", "dev"), None, None),
        P(("grp", "dev"), None),
        P(("grp", "dev"), "sec", None),
        P(("grp", "dev"), None, "sec"),
        P(("grp", "dev")),
        P(("sec", "grp"), None, None),
        P(("sec", "grp"), "dev"),
        P(("sec", "grp"), "dev"),
        P("dev"),
        P("dev", None),
        P(("sec", "grp"), None),
        P(("sec", "grp"), None),
        P("grp", "dev", None, "sec"),
        P("grp", "sec", "dev"),
    )
    out_specs = P(("sec", "grp"), "dev")
    return jax.shard_map(body, mesh=mesh, in_specs=in_specs, out_specs=out_specs, check_vma=False)
```

```python
import functools

import jax
import jax.numpy as jnp
from jax import lax
from jax.experimental import pallas as pl
from jax.experimental.pallas import tpu as pltpu
from jax.sharding import PartitionSpec as P

score_scale = 0.07216878364870323
route_scale = 2.5
norm_eps = 1e-06
masked_floor = -1e30
f32 = jnp.float32
bf16 = jnp.bfloat16


def spread(value, axis):
    copies = jnp.broadcast_to(value[None], (lax.axis_size(axis),) + value.shape)
    return lax.all_to_all(copies, axis, split_axis=0, concat_axis=0, tiled=True)


def in_vmem(count):
    return [pl.BlockSpec(memory_space=pltpu.VMEM) for _ in range(count)]


def iota(shape, axis):
    return lax.broadcasted_iota(jnp.int32, shape, axis)


def one_hot(condition):
    return jnp.where(condition, 1.0, 0.0).astype(bf16)


def select_rows(selection, rows):
    return jnp.dot(selection, rows, preferred_element_type=f32).astype(bf16)


def dot_nt(left, right):
    return lax.dot_general(left, right, (((1,), (1,)), ((), ())), preferred_element_type=f32)


def pad_lanes(value):
    spare = -value.shape[1] % 128
    if spare == 0:
        return value
    return jnp.concatenate([value, jnp.zeros((value.shape[0], spare), value.dtype)], axis=1)


def pack_slots(upper, lower):
    half = upper.shape[1] // 2
    last = jnp.where(
        iota((8, half), 0) < 4, lower[:, :half], pltpu.roll(lower[:, half:], 4, 0)
    )
    return jnp.concatenate([upper[:, :half], upper[:, half:], last], axis=0)


def unpack_slots(packed):
    last = packed[16:]
    upper = jnp.concatenate([packed[:8], packed[8:16]], axis=1)
    return upper, jnp.concatenate([last, pltpu.roll(last, 4, 0)], axis=1)


def pack_block(value):
    row = iota((8, 128), 0)
    tail = value[:, 384:]
    return jnp.concatenate(
        [
            jnp.where(row < 6, value[:, 128 * at : 128 * at + 128], pltpu.roll(tail, 6 - 2 * at, 0))
            for at in range(3)
        ],
        axis=0,
    )


def unpack_block(packed):
    row = iota((8, 128), 0)
    tiles = [packed[:8], packed[8:16], packed[16:]]
    turned = [pltpu.roll(tile, 2 * at + 2, 0) for at, tile in enumerate(tiles)]
    tail = jnp.where(row < 2, turned[0], jnp.where(row < 4, turned[1], turned[2]))
    return jnp.concatenate(tiles + [tail], axis=1)


def attend_kernel(
    place_ref,
    latent_hbm,
    rope_hbm,
    cache_hbm,
    cache_rope_hbm,
    sent_ref,
    kept_ref,
    latent_ref,
    rope_ref,
    cache_ref,
    cache_rope_ref,
    sems,
):
    copies = [
        pltpu.make_async_copy(source, target, sems.at[index])
        for index, (source, target) in enumerate(
            [
                (rope_hbm, rope_ref),
                (cache_rope_hbm, cache_rope_ref),
                (latent_hbm, latent_ref),
                (cache_hbm, cache_ref),
            ]
        )
    ]
    for copy in copies:
        copy.start()
    heads, latent = latent_ref.shape
    half = heads // 2
    width = cache_rope_ref.shape[0]
    mine = pl.multiple_of(place_ref[0] * half, half)
    other = pl.multiple_of(half - place_ref[0] * half, half)

    copies[0].wait()
    row = rope_ref[...].astype(f32)
    pairs = jnp.concatenate(
        [row[:, 128 * pair : 128 * pair + 128] for pair in range(heads * width // 128)], axis=0
    )
    head = iota((heads, heads // 2), 0) + jnp.where(
        iota((heads, heads // 2), 0) < half, other, mine - half
    )
    picked = select_rows(one_hot(head >> 1 == iota((heads, heads // 2), 1)), pairs.astype(bf16))
    lane_half = iota((heads, 128), 1) >> 6
    picked = jnp.where(lane_half == (iota((heads, 128), 0) & 1), picked, jnp.zeros_like(picked))
    copies[1].wait()
    keys = cache_rope_ref[...]
    rope_scores = jnp.dot(
        picked, jnp.concatenate([keys, keys], axis=0), preferred_element_type=f32
    )
    copies[2].wait()
    query = jnp.concatenate([latent_ref[pl.ds(other, half), :], latent_ref[pl.ds(mine, half), :]], axis=0)
    copies[3].wait()
    cache = cache_ref[...]
    scores = dot_nt(query, cache) + rope_scores
    usable = iota(scores.shape, 1) < place_ref[1]
    masked = jnp.where(usable, scores * score_scale, masked_floor)
    top = jnp.max(masked, axis=1, keepdims=True).astype(bf16).astype(f32)
    expon = jnp.where(usable, jnp.exp(masked - top), 0.0)
    mass = jnp.sum(expon, axis=1, keepdims=True)
    weighted = jnp.dot(expon.astype(bf16), cache, preferred_element_type=f32)
    mass_high = mass.astype(bf16).astype(f32)
    lane = iota((heads, 128), 1)
    side = jnp.where(lane == 0, top, 0.0)
    side = jnp.where(lane == 1, mass_high, side)
    side = jnp.where(lane == 2, mass - mass_high, side)
    kept_ref[:, :latent] = weighted[half:]
    kept_ref[:, latent:] = side[half:]
    sent_ref[:, :latent] = weighted[:half].astype(bf16)
    sent_ref[:, latent:] = side[:half].astype(bf16)


def half_sum_kernel(section_ref, both_ref, kept_ref, out_ref):
    theirs = jnp.where(section_ref[...] == 0, both_ref[1].astype(f32), both_ref[0].astype(f32))
    out_ref[...] = (kept_ref[...] + theirs).astype(bf16)


def last_sum_kernel(returned_ref, placement_ref, hidden_ref, out_ref):
    width = out_ref.shape[1]
    returned = returned_ref[...].reshape(-1, 128)
    tiles = jnp.dot(placement_ref[...], returned, preferred_element_type=f32)
    mixture = jnp.concatenate([tiles[8 * at : 8 * at + 8] for at in range(4)], axis=1)
    out_ref[...] = (hidden_ref[...] + mixture)[:, :width].astype(bf16)


def dispatch_kernel(
    expert_total, capacity, partial_ref, resid_ref, gain_ref, router_ref, routes_ref, slots_ref, buffer_ref, hidden_ref, placement_ref
):
    routes = routes_ref[...].astype(f32)
    slots = slots_ref[...].astype(f32)
    rows, choices = routes.shape
    chunk = buffer_ref.shape[1]
    lane = iota((rows, 128), 1)
    spot = iota((rows, expert_total * chunk), 1).astype(f32)
    named = jnp.zeros((rows, 128), f32)
    sources = [jnp.zeros(spot.shape, f32) for _ in range(4)]
    for choice in range(choices):
        route = routes[:, choice : choice + 1]
        slot = slots[:, choice : choice + 1]
        named = jnp.where(lane.astype(f32) == route, 1.0, named)
        pair = jnp.floor(slot * 0.5)
        wanted = [8.0 * at + slot for at in range(3)] + [6.0 * pair + 6.0 + slot]
        for at in range(4):
            place = jnp.where(slot < capacity, route * chunk + wanted[at], -1.0)
            sources[at] = jnp.where(spot == place, 1.0, sources[at])
    placement = jnp.concatenate(sources, axis=0).astype(bf16)
    placement_ref[...] = placement

    hidden = pad_lanes(resid_ref[...].astype(f32))
    for group in range(partial_ref.shape[0]):
        hidden = hidden + partial_ref[group].astype(f32)
    hidden_ref[...] = hidden
    width = gain_ref.shape[1]
    gained = hidden * pad_lanes(gain_ref[...])
    squares = jnp.sum(hidden * hidden, axis=1, keepdims=True)
    square_high = squares.astype(bf16).astype(f32)
    logits = lax.dot_general(
        gained[:, :width],
        router_ref[...],
        (((1,), (1,)), ((), ())),
        preferred_element_type=f32,
        precision=lax.Precision.HIGHEST,
    )
    spread_out = pad_lanes(logits)
    logit_high = spread_out.astype(bf16).astype(f32)
    first = width % 128
    side = pltpu.roll(logit_high, first, 1) + pltpu.roll(
        spread_out - logit_high, first + expert_total, 1
    )
    side = side + pltpu.roll(named, first + 2 * expert_total, 1)
    side = jnp.where(lane == first + 3 * expert_total, square_high, side)
    side = jnp.where(lane == first + 3 * expert_total + 1, squares - square_high, side)
    full = width - first
    last = jnp.where(lane < first, gained[:, full:], side)
    content = jnp.concatenate([gained[:, :full], last], axis=1)
    content = jnp.concatenate([content[:, 128 * at : 128 * at + 128] for at in range(4)], axis=0)
    out = lax.dot_general(
        placement, content.astype(bf16), (((0,), (0,)), ((), ())), preferred_element_type=f32
    )
    buffer_ref[...] = out.astype(bf16).reshape(buffer_ref.shape)


def project_kernel(section_ref, gathered_ref, weight_ref, sent_ref, kept_ref):
    members, groups, width = gathered_ref.shape
    total = members * groups
    rows = gathered_ref[...].reshape(total, width)
    target = iota((total, total), 0)
    source = iota((total, total), 1)
    wanted = (target >> 3 & 1) * (total // 2) + (target >> 4) * 8 + (target & 7)
    found = (source & (groups - 1)) * members + (source >> 4)
    rows = select_rows(one_hot(wanted == found), rows)
    out = dot_nt(rows, weight_ref[...])
    is_first = section_ref[...] == 0
    for owner in range(sent_ref.shape[0]):
        start = 16 * owner
        first = pad_lanes(out[start : start + 8])
        second = pad_lanes(out[start + 8 : start + 16])
        sent_ref[owner] = jnp.where(is_first, second, first).astype(bf16)
        kept_ref[owner] = jnp.where(is_first, first, second)


def gate_up_kernel(expert_total, expert_ref, received_ref, weight_ref, out_ref):
    members = received_ref.shape[1]
    width = 4 * received_ref.shape[3]
    row = iota((8, width), 0)
    rows, side = [], []
    first = iota((8, 128), 1) < 64
    is_expert = (iota((8, 128), 1) & 63) == 3 * expert_total + 2
    expert = expert_ref[...].astype(f32)
    for member in range(members):
        first_block = unpack_block(received_ref[0, member].astype(f32))
        turned = pltpu.roll(unpack_block(received_ref[1, member].astype(f32)), 6, 0)
        early = jnp.where(row < 6, first_block, turned)
        late = jnp.where(row < 4, turned, 0.0)
        rows += [early, late]
        turned = pltpu.roll(early[:, width - 128 :], 64, 1)
        last = jnp.where(first, turned, late[:, width - 128 :])
        side.append(jnp.where(is_expert, expert, last))
    left = jnp.concatenate(rows, axis=0).astype(bf16)
    gate = jnp.dot(left, weight_ref[:width, :], preferred_element_type=f32)
    up = jnp.dot(left, weight_ref[width:, :], preferred_element_type=f32)
    unit = gate.shape[1]
    over = iota((8, unit), 0) < 4
    for member in range(members):
        start = 16 * member
        late_up = pltpu.roll(up[start + 8 : start + 16], 4, 0)
        blocks = [
            gate[start : start + 8],
            jnp.where(over, gate[start + 8 : start + 16], late_up),
            up[start : start + 8],
        ]
        tiles = [block[:, at : at + 128] for block in blocks for at in range(0, unit, 128)]
        out_ref[member] = jnp.concatenate(tiles + [side[member]], axis=0).astype(bf16)


def activate_kernel(model_width, expert_total, sums_ref, out_ref):
    members, height, _ = sums_ref.shape
    columns = height // 24
    total = sums_ref[0].astype(f32)
    for member in range(1, members):
        total = total + sums_ref[member].astype(f32)

    def block(row):
        first = 8 * columns * row
        return jnp.concatenate(
            [total[first + 8 * col : first + 8 * col + 8] for col in range(columns)], axis=1
        )

    side = total[24 * columns :]
    side = jnp.concatenate([side, pltpu.roll(side, 64, 1)], axis=0)
    lane = iota(side.shape, 1)
    logits = side + pltpu.roll(side, 128 - expert_total, 1)
    named = pltpu.roll(side, 128 - 2 * expert_total, 1)
    square_lane = 3 * expert_total
    is_square = (lane == square_lane) | (lane == square_lane + 1)
    squares = jnp.sum(jnp.where(is_square, side, 0.0), axis=1, keepdims=True)
    inverse_rms = lax.rsqrt(squares / model_width + norm_eps)
    scores = 1.0 / (1.0 + jnp.exp(-jnp.where(lane < expert_total, logits * inverse_rms, 0.0)))
    chosen = (named > 0.5) & (lane < expert_total)
    expert = jnp.sum(jnp.where(lane == square_lane + 2, side, 0.0), axis=1, keepdims=True)
    is_own = lane.astype(f32) * members == expert
    picked = jnp.sum(jnp.where(is_own, scores, 0.0), axis=1, keepdims=True)
    denominator = jnp.sum(jnp.where(chosen, scores, 0.0), axis=1, keepdims=True)
    occupied = denominator > 0.0
    weight = route_scale * picked / jnp.where(occupied, denominator, 1.0)
    weight = jnp.where(occupied, weight, 0.0)

    def activation(gate, up, scale, share):
        gate = gate * scale
        return gate / (1.0 + jnp.exp(-gate)) * (up * scale) * share

    early = activation(block(0), block(2), inverse_rms[:8], weight[:8])
    mixed = block(1)
    late = activation(mixed, pltpu.roll(mixed, 4, 0), inverse_rms[8:], weight[8:])
    packed = pack_slots(early, late).astype(bf16)
    for member in range(out_ref.shape[0]):
        out_ref[member] = packed


def down_kernel(section_ref, packed_ref, weight_ref, sent_ref, kept_ref):
    rows = []
    for member in range(packed_ref.shape[0]):
        rows += unpack_slots(packed_ref[member].astype(f32))
    left = jnp.concatenate(rows, axis=0).astype(bf16)
    out = pad_lanes(dot_nt(left, weight_ref[...]))
    is_first = section_ref[...] == 0
    for group in range(sent_ref.shape[0]):
        start = 16 * group
        early, late = out[start : start + 8], out[start + 8 : start + 16]
        row = iota(early.shape, 0)
        second = jnp.where(row < 2, pltpu.roll(early, 2, 0), pltpu.roll(late, 2, 0))
        first, second = pack_block(early), pack_block(second)
        sent_ref[group] = jnp.where(is_first, second, first).astype(bf16)
        kept_ref[group] = jnp.where(is_first, first, second)


def body(
    q_latent,
    q_rope,
    cache_latent,
    cache_rope,
    lengths,
    w_uv,
    w_out,
    resid,
    norm_gain,
    router,
    routes,
    slots,
    w_gateup,
    w_down,
):
    sections = lax.axis_size("sec")
    groups = lax.axis_size("grp")
    members = lax.axis_size("dev")
    section = lax.axis_index("sec")
    _, head_total, latent = q_latent.shape
    hist_local = cache_latent.shape[1]
    rope_width = cache_rope.shape[1]
    half_heads = head_total // sections
    head_block, _, value_width = w_uv.shape
    block_rows, width_local = resid.shape
    expert_total = router.shape[1]
    capacity = max(2, 3 * block_rows // 4)
    padded_width = width_local + -width_local % 128
    in_smem = pl.BlockSpec(memory_space=pltpu.SMEM)
    vmem = pltpu.CompilerParams(vmem_limit_bytes=32 * 2**20)

    own_section = section.reshape(1, 1)
    place = jnp.stack([section, lengths[0] - section * hist_local]).astype(jnp.int32)
    sent, kept_part = pl.pallas_call(
        attend_kernel,
        out_shape=(
            jax.ShapeDtypeStruct((half_heads, latent + 128), bf16),
            jax.ShapeDtypeStruct((half_heads, latent + 128), f32),
        ),
        in_specs=[in_smem] + [pl.BlockSpec(memory_space=pltpu.HBM)] * 4,
        out_specs=tuple(in_vmem(2)),
        scratch_shapes=[
            pltpu.VMEM((head_total, latent), bf16),
            pltpu.VMEM(q_rope.shape, bf16),
            pltpu.VMEM(cache_latent.shape[1:], bf16),
            pltpu.VMEM(cache_rope.shape[1:], bf16),
            pltpu.SemaphoreType.DMA((4,)),
        ],
        compiler_params=vmem,
    )(
        place,
        *[
            pltpu.with_memory_space_constraint(operand, pltpu.HBM)
            for operand in (q_latent[0], q_rope, cache_latent[0], cache_rope[0])
        ],
    )

    other = 1 - section
    both = lax.all_gather(sent, "sec", axis=0)
    theirs = lax.dynamic_index_in_dim(both, other, 0, False)
    top_mine = kept_part[:, latent : latent + 1]
    mass_mine = kept_part[:, latent + 1 : latent + 2] + kept_part[:, latent + 2 : latent + 3]
    top_theirs = theirs[:, latent : latent + 1].astype(f32)
    mass_theirs = (
        theirs[:, latent + 1 : latent + 2].astype(f32)
        + theirs[:, latent + 2 : latent + 3].astype(f32)
    )
    top_both = jnp.maximum(top_mine, top_theirs)
    factor_mine = jnp.exp(top_mine - top_both)
    factor_theirs = jnp.exp(top_theirs - top_both)
    mass_both = mass_mine * factor_mine + mass_theirs * factor_theirs
    latent_out = (
        kept_part[:, :latent] * factor_mine + theirs[:, :latent].astype(f32) * factor_theirs
    ) / mass_both
    latent_out = latent_out.astype(bf16)

    outgoing_heads = latent_out.reshape(groups, head_block, latent)
    arrived = lax.all_to_all(outgoing_heads, "grp", split_axis=0, concat_axis=0, tiled=True)
    values = jnp.einsum("nhc,hcv->nhv", arrived, w_uv, preferred_element_type=f32).astype(bf16)
    width_heads = head_block * value_width
    gathered = spread(values.reshape(groups, width_heads), "dev")
    sent, kept = pl.pallas_call(
        project_kernel,
        out_shape=(
            jax.ShapeDtypeStruct((groups, block_rows, padded_width), bf16),
            jax.ShapeDtypeStruct((groups, block_rows, padded_width), f32),
        ),
        in_specs=in_vmem(3),
        out_specs=tuple(in_vmem(2)),
        compiler_params=vmem,
    )(own_section, gathered, w_out.T)

    def sum_halves(sent, kept):
        return pl.pallas_call(
            half_sum_kernel,
            out_shape=jax.ShapeDtypeStruct(sent.shape, bf16),
            in_specs=in_vmem(3),
            out_specs=in_vmem(1)[0],
            compiler_params=vmem,
        )(own_section, lax.all_gather(sent, "sec", axis=0), kept)

    partial = sum_halves(sent, kept)
    partial = lax.all_to_all(partial, "grp", split_axis=0, concat_axis=0, tiled=True)

    buffer, hidden, placement = pl.pallas_call(
        functools.partial(dispatch_kernel, expert_total, capacity),
        out_shape=(
            jax.ShapeDtypeStruct((expert_total, 24, 128), bf16),
            jax.ShapeDtypeStruct((block_rows, padded_width), f32),
            jax.ShapeDtypeStruct((4 * block_rows, expert_total * 24), bf16),
        ),
        in_specs=in_vmem(6),
        out_specs=tuple(in_vmem(3)),
        compiler_params=vmem,
    )(partial, resid, norm_gain[None], router.T, routes, slots)
    received = lax.all_to_all(buffer, "grp", split_axis=0, concat_axis=0, tiled=True)
    received = lax.all_gather(received, "sec", axis=0)

    unit = w_gateup.shape[3]
    weight = jnp.pad(
        w_gateup[0].transpose(1, 0, 2), ((0, 0), (0, padded_width - width_local), (0, 0))
    ).reshape(2 * padded_width, unit)
    sums = pl.pallas_call(
        functools.partial(gate_up_kernel, expert_total),
        out_shape=jax.ShapeDtypeStruct((members, 24 * unit // 128 + 8, 128), bf16),
        in_specs=in_vmem(3),
        out_specs=in_vmem(1)[0],
        compiler_params=vmem,
    )(lax.axis_index("grp").reshape(1, 1), received, weight)
    sums = lax.all_to_all(sums, "dev", split_axis=0, concat_axis=0, tiled=True)
    packed = pl.pallas_call(
        functools.partial(activate_kernel, width_local * members, expert_total),
        out_shape=jax.ShapeDtypeStruct((members, 24, unit // 2), bf16),
        in_specs=in_vmem(1),
        out_specs=in_vmem(1)[0],
        compiler_params=vmem,
    )(sums)

    everyone = lax.all_to_all(packed, "dev", split_axis=0, concat_axis=0, tiled=True)
    sent, kept = pl.pallas_call(
        down_kernel,
        out_shape=(
            jax.ShapeDtypeStruct((groups, 24, 128), bf16),
            jax.ShapeDtypeStruct((groups, 24, 128), f32),
        ),
        in_specs=in_vmem(3),
        out_specs=tuple(in_vmem(2)),
        compiler_params=vmem,
    )(own_section, everyone, w_down[0].T)
    down = sum_halves(sent, kept)
    returned = lax.all_to_all(down, "grp", split_axis=0, concat_axis=0, tiled=True)
    return pl.pallas_call(
        last_sum_kernel,
        out_shape=jax.ShapeDtypeStruct((block_rows, width_local), bf16),
        in_specs=in_vmem(3),
        out_specs=in_vmem(1)[0],
        compiler_params=vmem,
    )(returned, placement, hidden)


def solution(mesh):
    in_specs = (
        P(("grp", "dev"), None, None),
        P(("grp", "dev"), None),
        P(("grp", "dev"), "sec", None),
        P(("grp", "dev"), None, "sec"),
        P(("grp", "dev")),
        P(("sec", "grp"), None, None),
        P(("sec", "grp"), "dev"),
        P(("sec", "grp"), "dev"),
        P("dev"),
        P("dev", None),
        P(("sec", "grp"), None),
        P(("sec", "grp"), None),
        P("grp", "dev", None, "sec"),
        P("grp", "sec", "dev"),
    )
    out_specs = P(("sec", "grp"), "dev")
    return jax.shard_map(body, mesh=mesh, in_specs=in_specs, out_specs=out_specs, check_vma=False)
```
